128 devices in a mesh: ctx: 16 (over x, z), head: 8 (over y, core).
Axes of the slice: x: 4, y: 4, z: 4, core: 2. Of those that a mesh axis runs over, the one named last changes fastest.
Arguments:
- queries: bfloat16 [8192, 4096], P('ctx', 'head'), may hold values from -6 to 6
- key_states: bfloat16 [8192, 4096], P('ctx', 'head'), may hold values from -6 to 6
- value_states: bfloat16 [8192, 4096], P('ctx', 'head'), may hold values from -6 to 6
- transition_vectors: bfloat16 [8192, 4096], P('ctx', 'head'), may hold values from -6 to 6
- beta_logit: float32 [8192, 32], P('ctx', 'head'), may hold values from -6 to 6
- document_ids: int32 [8192], P('ctx'), may hold values from 0 to 7, as said below
- out_weight: bfloat16 [4096, 4096], P('head'), may hold values from -0.09375 to 0.09375
Outputs:
- layer_out: bfloat16 [8192, 4096], P(('ctx', 'head'))
The draws below stay inside these ranges and needn't reach their ends.
Inputs may be any that keep to these rules, and one draw needn't show every extreme that they name: `document_ids`: document ids never fall along the sequence; document 0 is the first 4352 tokens; the other documents have 1 or more tokens each and together fill the rest.
All inputs are finite; a program needn't handle non-finite values.
Results may differ from the reference program's by a relative error of at most 0.022.
Values may be sent and summed in bfloat16 or wider, within the bound.
A program may use at most 128 MiB of HBM per device.

```python
import jax
import jax.numpy as jnp
from jax import lax

HEADS = 32
DH = 128
D = 4096
TOK_DEV = 512
TOKENS = 8192
N_CTX = 16


def draw_queries(key, part):
    drawn = jnp.clip(jax.random.normal(jax.random.fold_in(key, 11), (TOKENS, HEADS * DH), jnp.float32), -6.0, 6.0)
    return drawn.astype(jnp.bfloat16)


def draw_key_states(key, part):
    drawn = jnp.clip(jax.random.normal(jax.random.fold_in(key, 12), (TOKENS, HEADS * DH), jnp.float32), -6.0, 6.0)
    return drawn.astype(jnp.bfloat16)


def draw_beta_logit(key, part):
    sign_values = 2.0 * jax.random.randint(jax.random.fold_in(key, 14), (TOKENS, HEADS), 0, 2).astype(jnp.float32) - 1.0
    magnitude = jax.random.uniform(jax.random.fold_in(key, 13), (TOKENS, HEADS), jnp.float32, 4.75, 6.0)
    drawn = sign_values * magnitude
    return drawn.astype(jnp.float32)


def draw_document_ids(key, part):
    first_length = TOKENS // 2 + TOK_DEV // 2
    rest_length = TOKENS - first_length
    seeded = jax.random.fold_in(key, 5209)
    cut_points = jax.random.permutation(seeded, rest_length - 1)[:6].astype(jnp.int32) + 1
    positions = jnp.arange(TOKENS, dtype=jnp.int32)
    offsets = positions - first_length
    later = 1 + jnp.sum((cut_points[None, :] <= offsets[:, None]).astype(jnp.int32), axis=1)
    return jnp.where(positions < first_length, 0, later).astype(jnp.int32)


def block_levels(stream_key, shape, pieces, least, top_value):
    def one(dim, parts):
        draws = jax.random.uniform(jax.random.fold_in(jax.random.fold_in(stream_key, 6), dim), (parts,), jnp.float32, least / len(pieces), top_value / len(pieces))
        return jnp.repeat(jnp.exp(draws), shape[dim] // parts).reshape((-1,) + (1,) * (len(shape) - dim - 1))

    level = one(*pieces[0])
    for cut in pieces[1:]:
        level = level * one(*cut)
    return level


def gaussian(rng, dims, width, bound, split=(), kind=jnp.bfloat16):
    values = width * jax.random.normal(rng, dims, jnp.float32)
    if split:
        values = values * block_levels(rng, dims, split, -0.22, 0.18)
    return jnp.clip(values, -bound, bound).astype(kind)


def setup_inputs(seed: int = 0) -> dict:
    key_list = jax.random.split(jax.random.key(seed), 8)
    queries = draw_queries(jax.random.fold_in(key_list[7], 71), 0)
    key_states = draw_key_states(jax.random.fold_in(key_list[7], 71), 0)
    value_states = gaussian(key_list[2], (TOKENS, D), 1.0, 6.0, ((0, 16), (1, 8)))
    transition_vectors = gaussian(key_list[3], (TOKENS, D), 1.0, 6.0, ((0, 16), (1, 8)))
    beta_logit = draw_beta_logit(jax.random.fold_in(key_list[7], 71), 0)
    document_ids = draw_document_ids(jax.random.fold_in(key_list[7], 71), 0)
    out_weight = gaussian(key_list[6], (D, D), D ** -0.5, 0.09375, ((0, 8),))
    return dict(queries=queries, key_states=key_states, value_states=value_states, transition_vectors=transition_vectors, beta_logit=beta_logit, document_ids=document_ids, out_weight=out_weight)


epsilon = 1e-06
masked_value = -1e+30
highest = lax.Precision.HIGHEST

def shard_operators(query_block, key_block, vector_block, strength):
    block_rows = key_block.shape[0]
    head_width = key_block.shape[1]
    row_ids = jnp.arange(block_rows)
    strict = row_ids[:, None] > row_ids[None, :]
    causal = row_ids[:, None] >= row_ids[None, :]
    intersections = jnp.dot(vector_block, vector_block.T, precision=highest)
    unit_lower = jnp.where(strict, intersections * strength[None, :], 0.0) + jnp.eye(block_rows, dtype=jnp.float32)
    key_proj = jnp.where(strict, jnp.dot(vector_block, key_block.T, precision=highest), 0.0)
    solved = lax.linalg.triangular_solve(unit_lower, jnp.concatenate([key_proj, vector_block], axis=1), left_side=True, lower=True, unit_diagonal=True)
    key_solve = solved[:, :block_rows]
    vector_solve = solved[:, block_rows:]
    weighted = strength[:, None] * vector_block
    keys_end = (key_block - jnp.dot(key_solve.T, weighted, precision=highest)).astype(jnp.bfloat16)
    transfer = jnp.eye(head_width, dtype=jnp.float32) - jnp.dot(vector_block.T, strength[:, None] * vector_solve, precision=highest)
    query_dots = jnp.where(causal, jnp.dot(query_block, vector_block.T, precision=highest), 0.0)
    scaled_dots = query_dots * strength[None, :]
    intra_scores = jnp.dot(query_block, key_block.T, precision=highest) - jnp.dot(scaled_dots, key_solve, precision=highest)
    rotated = query_block - jnp.dot(scaled_dots, vector_solve, precision=highest)
    return (intra_scores, keys_end, transfer, rotated)

def one_head(operands, document_ids):
    query_head, key_head, value_head, vector_head, logit_head = operands
    block_rows = TOK_DEV
    head_width = query_head.shape[1]
    score_scale = head_width ** (-0.5)
    strength = 2.0 * jax.nn.sigmoid(logit_head)
    vector_float = vector_head.astype(jnp.float32)
    unit_vectors = vector_float / jnp.sqrt(lax.optimization_barrier(jnp.sum(vector_float * vector_float, axis=1, keepdims=True)) + epsilon)
    row_ids = jnp.arange(block_rows)
    causal = row_ids[:, None] >= row_ids[None, :]
    operators = []
    for anchor in range(N_CTX):
        lower_end = anchor * block_rows
        upper_end = lower_end + block_rows
        operators.append(shard_operators(query_head[lower_end:upper_end].astype(jnp.float32), key_head[lower_end:upper_end].astype(jnp.float32), unit_vectors[lower_end:upper_end], strength[lower_end:upper_end]))
    results = []
    for target in range(N_CTX):
        query_docs = document_ids[target * block_rows:(target + 1) * block_rows]
        intra_scores, keys_end, transfer, rotated = operators[target]
        allowed = causal & (query_docs[:, None] == query_docs[None, :])
        blocks = [jnp.where(allowed, intra_scores * score_scale, masked_value)]
        value_parts = [value_head[target * block_rows:(target + 1) * block_rows]]
        for anchor in range(target - 1, -1, -1):
            key_docs = document_ids[anchor * block_rows:(anchor + 1) * block_rows]
            scores = jnp.dot(rotated.astype(jnp.bfloat16).astype(jnp.float32), operators[anchor][1].T.astype(jnp.float32), preferred_element_type=jnp.float32)
            blocks.append(jnp.where(query_docs[:, None] == key_docs[None, :], scores * score_scale, masked_value))
            value_parts.append(value_head[anchor * block_rows:(anchor + 1) * block_rows])
            rotated = jnp.dot(rotated, operators[anchor][2], precision=highest)
        scores = jnp.concatenate(blocks, axis=1)
        row_max = lax.optimization_barrier(jnp.max(scores, axis=1, keepdims=True))
        weights = jnp.exp(scores - row_max)
        row_total = lax.optimization_barrier(jnp.sum(weights, axis=1, keepdims=True))
        mixed = jnp.dot(weights.astype(jnp.bfloat16).astype(jnp.float32), jnp.concatenate(value_parts, axis=0).astype(jnp.float32), preferred_element_type=jnp.float32)
        results.append((mixed / row_total).astype(jnp.bfloat16))
    return jnp.concatenate(results, axis=0)

def reference(queries, key_states, value_states, transition_vectors, beta_logit, document_ids, out_weight):

    def split_heads(flat):
        return jnp.transpose(flat.reshape(TOKENS, HEADS, DH), (1, 0, 2))
    per_head = lax.map(lambda operands: one_head(operands, document_ids), (split_heads(queries), split_heads(key_states), split_heads(value_states), split_heads(transition_vectors), beta_logit.T))
    attended = jnp.transpose(per_head, (1, 0, 2)).reshape(TOKENS, HEADS * DH)
    return jnp.dot(attended.astype(jnp.float32), out_weight.astype(jnp.float32), preferred_element_type=jnp.float32).astype(jnp.bfloat16)
```

```python
import functools
import math

import jax
import jax.numpy as jnp
from jax import lax
from jax.experimental import pallas as pl
from jax.experimental.pallas import tpu as pltpu
from jax.sharding import PartitionSpec as P

MESH = pl.DeviceIdType.MESH
F32 = jnp.float32
BF16 = jnp.bfloat16

HEAD = 128
BLOCK = 512
SUB = 128
N_SUB = 4
N_HEAD = 4
GROUP = 4
TILE = 256
NEG = -1e30
UNIT = math.log2(math.e) / math.sqrt(HEAD)

AT_Q, AT_K, AT_V, AT_T, AT_D = 0, 512, 1024, 1536, 1664
PACKET = 1680
PART = BLOCK + 16
PART_HALF = TILE + 16


def nn(a, b):
    return lax.dot_general(a, b, (((1,), (0,)), ((), ())), preferred_element_type=F32)


def nt(a, b):
    return lax.dot_general(a, b, (((1,), (1,)), ((), ())), preferred_element_type=F32)


def halves(a):
    high = a.astype(BF16)
    return high, (a - high.astype(F32)).astype(BF16)


def rows_to_column(row, eye):
    return jnp.sum(jnp.where(eye, row, 0.0), axis=1, keepdims=True)


def column_to_rows(column, eye):
    return jnp.sum(jnp.where(eye, column, 0.0), axis=0, keepdims=True)


def pieces(rows):
    high = rows.astype(BF16).astype(F32)
    rest = rows - high
    middle = rest.astype(BF16).astype(F32)
    low = rest - middle
    pad = jnp.zeros((16 - 3 * rows.shape[0], rows.shape[1]), F32)
    return jnp.concatenate([high, middle, low, pad], axis=0).astype(BF16)


def unpieced(tail, count):
    tail = tail.astype(F32)
    return tail[:count] + tail[count : 2 * count] + tail[2 * count : 3 * count]


def identity_masks():
    row = lax.broadcasted_iota(jnp.int32, (SUB, SUB), 0)
    col = lax.broadcasted_iota(jnp.int32, (SUB, SUB), 1)
    return row, col


def attention_kernel(
    q_ref, k_ref, v_ref, u_ref, logit_ref, doc_ref, out_ref,
    level_ref, beta_ref, packet_out, packet_in, turned_ref, forward_ref, cross_in, lone_in, lone_out,
    part_in_out, part_cross_out, part_lone_out, part_in, part_cross, part_lone, log_ref,
    acc_ref, max_ref, sum_ref,
    own_sem, pk_send, pk_recv, xf_send, xf_recv, lone_send, lone_recv,
    pi_send, pi_recv, pc_send, pc_recv, pl_send, pl_recv,
):
    me = lax.axis_index("ctx")
    n_ctx = lax.axis_size("ctx")
    x = me // GROUP
    z = lax.rem(me, GROUP)
    base = x * GROUP

    barrier = pltpu.get_barrier_semaphore()

    def greet(step, carry):
        pl.semaphore_signal(barrier, inc=1, device_id={"ctx": lax.rem(me + step, n_ctx)}, device_id_type=MESH)
        return carry

    lax.fori_loop(1, n_ctx, greet, 0)

    row, col = identity_masks()
    for level in range(7):
        hit = ((row >> level) + 1 == (col >> level)) & (((row >> level) & 1) == 0)
        level_ref[level] = jnp.where(hit, 1.0, 0.0).astype(BF16)
    beta_ref[...] = 2.0 * jax.nn.sigmoid(logit_ref[...])

    def send_packet(head):
        return pltpu.make_async_remote_copy(
            src_ref=packet_out.at[head], dst_ref=packet_in.at[z],
            send_sem=pk_send.at[head], recv_sem=pk_recv.at[z],
            device_id={"ctx": base + head}, device_id_type=MESH,
        )

    def head_step(turn, carry):
        head = lax.rem(z + 1 + turn, N_HEAD)
        lanes = pl.ds(pl.multiple_of(head * HEAD, HEAD), HEAD)
        row, col = identity_masks()
        eye = row == col
        upper = col > row
        lower = col < row
        causal = col <= row
        one = jnp.where(eye, 1.0, 0.0)
        lane4 = lax.broadcasted_iota(jnp.int32, (BLOCK, N_HEAD), 1)
        beta = jnp.sum(jnp.where(lane4 == head, beta_ref[...], 0.0), axis=1, keepdims=True)
        subs = range(N_SUB)
        at = [slice(a * SUB, (a + 1) * SUB) for a in subs]
        q = [q_ref[at[a], lanes] for a in subs]
        k = [k_ref[at[a], lanes] for a in subs]
        v = [v_ref[at[a], lanes] for a in subs]
        u = [u_ref[at[a], lanes] for a in subs]
        tau, tau_row, lt, low_t, lt_low, skew_t, qk, skew, aq = [], [], [], [], [], [], [], [], []
        for a in subs:
            wide = u[a].astype(F32)
            tau.append(beta[at[a]] / (jnp.sum(wide * wide, axis=1, keepdims=True) + 1e-6))
            tau_row.append(column_to_rows(tau[a], eye))
            gram = jnp.where(upper, nt(u[a], u[a]) * tau[a], 0.0)
            high, low = halves(gram)
            lt.append(high)
            lt_low.append(low)
        inverse = []
        for a in subs:
            inverse.append((one - (lt[a] * level_ref[0]).astype(F32)).astype(BF16))
        for level in range(1, 7):
            first = [nn(inverse[a], lt[a] * level_ref[level]).astype(BF16) for a in subs]
            inverse = [
                (inverse[a].astype(F32) - nn(first[a], inverse[a])).astype(BF16) for a in subs
            ]
        residual = [
            (one - inverse[a].astype(F32) - (nn(lt[a], inverse[a]) + nn(lt_low[a], inverse[a]))).astype(BF16)
            for a in subs
        ]
        solved = [inverse[a].astype(F32) + nn(inverse[a], residual[a]) for a in subs]
        z_full, trans, keys, intra, turned = [], [], [], [], []
        for a in subs:
            high, low = halves(solved[a] * tau_row[a])
            z_full.append(nn(high, u[a]) + nn(low, u[a]))
        for a in subs:
            high, low = halves(z_full[a])
            across = u[a].astype(F32).T.astype(BF16)
            trans.append(one - (nn(across, high) + nn(across, low)))
            skew_t = jnp.where(upper, nt(k[a], u[a]), 0.0).astype(BF16)
            keys.append(k[a].astype(F32) - nn(skew_t, high))
        for a in subs:
            a_high, a_low = halves(jnp.where(causal, nt(q[a], u[a]), 0.0) * tau_row[a])
            s_high, s_low = halves(solved[a])
            y = (nt(a_high, s_high) + nt(a_low, s_high) + nt(a_high, s_low)).astype(BF16)
            skew = jnp.where(lower, nt(u[a], k[a]), 0.0).astype(BF16)
            intra.append((nt(q[a], k[a]) - nn(y, skew)) * UNIT)
            turned.append((q[a].astype(F32) - nn(y, u[a])) * UNIT)

        def as_b(value):
            return value.astype(BF16)

        t_b = [as_b(trans[a]) for a in subs]
        near_10 = nt(as_b(turned[1]), as_b(keys[0]))
        near_32 = nt(as_b(turned[3]), as_b(keys[2]))
        turned[1] = nt(as_b(turned[1]), t_b[0])
        turned[3] = nt(as_b(turned[3]), t_b[2])
        keys[0] = nn(as_b(keys[0]), t_b[1])
        keys[2] = nn(as_b(keys[2]), t_b[3])

        def product(left, right):
            left_high, left_low = halves(left)
            right_high, right_low = halves(right)
            return nn(left_high, right_high) + nn(left_low, right_high) + nn(left_high, right_low)

        pair_a = product(trans[0], trans[1])
        pair_b = product(trans[2], trans[3])
        late = jnp.concatenate([as_b(turned[2]), as_b(turned[3])], axis=0)
        early = jnp.concatenate([as_b(keys[0]), as_b(keys[1])], axis=0)
        far = nt(late, early)
        late = nt(late, as_b(pair_a))
        early = nn(early, as_b(pair_b))
        whole = product(pair_a, pair_b)
        packet_out[head, AT_Q : AT_Q + 256] = as_b(jnp.concatenate([turned[0], turned[1]], axis=0))
        packet_out[head, AT_Q + 256 : AT_Q + 512] = as_b(late)
        packet_out[head, AT_K : AT_K + 256] = as_b(early)
        packet_out[head, AT_K + 256 : AT_K + 512] = as_b(jnp.concatenate([keys[2], keys[3]], axis=0))
        packet_out[head, AT_V : AT_V + 512] = jnp.concatenate(v, axis=0)
        packet_out[head, AT_T : AT_T + 128] = as_b(whole)
        docs = doc_ref[...]
        packet_out[head, AT_D : AT_D + 16] = as_b(
            jnp.concatenate([docs, jnp.zeros((16 - N_SUB, SUB), F32)], axis=0)
        )

        @pl.when(turn == 0)
        def _():
            pl.semaphore_wait(barrier, n_ctx - 1)

        @pl.when(turn < N_HEAD - 1)
        def _():
            send_packet(head).start()

        tiles = [
            [intra[0]],
            [near_10, intra[1]],
            [far[:SUB, :SUB], far[:SUB, SUB:], intra[2]],
            [far[SUB:, :SUB], far[SUB:, SUB:], near_32, intra[3]],
        ]
        for a in subs:
            mine = rows_to_column(docs[a : a + 1], eye)
            scores = []
            for b in range(a + 1):
                allowed = mine == docs[b : b + 1]
                if b == a:
                    allowed = allowed & causal
                scores.append(jnp.where(allowed, tiles[a][b], NEG))
            top = scores[0]
            for score in scores[1:]:
                top = jnp.maximum(top, score)
            top = jnp.max(top, axis=1, keepdims=True)
            weights = [jnp.exp2(score - top) for score in scores]
            total = weights[0]
            for weight in weights[1:]:
                total = total + weight
            total = jnp.sum(total, axis=1, keepdims=True)
            joined = jnp.concatenate([as_b(weight) for weight in weights], axis=1)
            acc_ref[head, at[a]] = nn(joined, jnp.concatenate(v[: a + 1], axis=0))
            max_ref[head, at[a]] = jnp.broadcast_to(top, (SUB, HEAD))
            sum_ref[head, at[a]] = jnp.broadcast_to(total, (SUB, HEAD))
        return carry

    lax.fori_loop(0, N_HEAD, head_step, 0)

    own = pltpu.make_async_copy(packet_out.at[z], packet_in.at[z], own_sem)
    own.start()
    own.wait()

    def packet_arrival(slot):
        return pltpu.make_async_remote_copy(
            src_ref=packet_out.at[slot], dst_ref=packet_in.at[slot],
            send_sem=pk_send.at[slot], recv_sem=pk_recv.at[slot],
            device_id={"ctx": base + slot}, device_id_type=MESH,
        )

    for slot in range(GROUP):
        @pl.when(slot != z)
        def _():
            packet_arrival(slot).wait_recv()

    def transition(slot):
        return packet_in[slot, AT_T : AT_T + 128]

    def send_forward(slot):
        return pltpu.make_async_remote_copy(
            src_ref=forward_ref.at[slot], dst_ref=cross_in.at[slot],
            send_sem=xf_send.at[slot], recv_sem=xf_recv.at[slot],
            device_id={"ctx": lax.rem(me + n_ctx - GROUP, n_ctx)}, device_id_type=MESH,
        )

    def send_lone():
        return pltpu.make_async_remote_copy(
            src_ref=lone_out, dst_ref=lone_in,
            send_sem=lone_send, recv_sem=lone_recv,
            device_id={"ctx": lax.rem(me + n_ctx - GROUP, n_ctx)}, device_id_type=MESH,
        )

    @pl.when(x == 2)
    def _():
        lone_out[...] = packet_in[0, AT_Q : AT_Q + TILE]
        send_lone().start()

    is_odd = lax.rem(x, 2) == 1
    for slot in range(GROUP):
        value = packet_in[slot, AT_Q : AT_Q + BLOCK]
        for source in range(slot - 1, -1, -1):
            turned_ref[slot * (slot - 1) // 2 + source] = value
            if source > 0:
                value = nt(value, transition(source)).astype(BF16)

        @pl.when(is_odd)
        def _():
            last = value if slot == 0 else nt(value, transition(0)).astype(BF16)
            forward_ref[slot, 0:BLOCK] = last
            forward_ref[slot, BLOCK:] = packet_in[slot, AT_D : AT_D + 16]
            send_forward(slot).start()

    row, col = identity_masks()
    eye = row == col

    def key_documents(slot):
        docs = packet_in[slot, AT_D : AT_D + 16].astype(F32)
        return [docs[a : a + 1] for a in range(N_SUB)]

    def attend(turned, slots, query_docs):
        scores = []
        for value, slot in zip(turned, slots):
            raw = nt(value, packet_in[slot, AT_K : AT_K + BLOCK])
            for a, docs in enumerate(key_documents(slot)):
                scores.append(jnp.where(query_docs == docs, raw[:, a * SUB : (a + 1) * SUB], NEG))
        top = scores[0]
        for score in scores[1:]:
            top = jnp.maximum(top, score)
        top = jnp.max(top, axis=1, keepdims=True)
        total = None
        mixed = None
        for index, slot in enumerate(slots):
            weights = [jnp.exp2(score - top) for score in scores[index * N_SUB : (index + 1) * N_SUB]]
            for weight in weights:
                total = weight if total is None else total + weight
            joined = jnp.concatenate([weight.astype(BF16) for weight in weights], axis=1)
            term = nn(joined, packet_in[slot, AT_V : AT_V + BLOCK])
            mixed = term if mixed is None else mixed + term
        total = jnp.sum(total, axis=1, keepdims=True)
        return (mixed / total).astype(BF16), top + jnp.log2(total)

    def query_documents(docs, tile):
        columns = [rows_to_column(docs[a : a + 1], eye) for a in range(2)]
        return jnp.concatenate(columns, axis=0)

    def log_rows(log_sum):
        return jnp.concatenate(
            [column_to_rows(log_sum[a * SUB : (a + 1) * SUB], eye) for a in range(2)], axis=0
        )

    def send_part_in(slot):
        return pltpu.make_async_remote_copy(
            src_ref=part_in_out.at[slot], dst_ref=part_in.at[z],
            send_sem=pi_send.at[slot], recv_sem=pi_recv.at[z],
            device_id={"ctx": base + slot}, device_id_type=MESH,
        )

    for slot in range(1, GROUP):
        docs = packet_in[slot, AT_D : AT_D + 16].astype(F32)
        logs = []
        for tile in range(BLOCK // TILE):
            at = slice(tile * TILE, (tile + 1) * TILE)
            sources = list(range(slot - 1, -1, -1))
            turned = [turned_ref[slot * (slot - 1) // 2 + source, at] for source in sources]
            mixed, log_sum = attend(turned, sources, query_documents(docs[2 * tile : 2 * tile + 2], tile))
            part_in_out[slot, at] = mixed
            logs.append(log_rows(log_sum))
        part_in_out[slot, BLOCK:] = pieces(jnp.concatenate(logs, axis=0))

        @pl.when(slot != z)
        def _():
            send_part_in(slot).start()

        @pl.when(slot == z)
        def _():
            part_in[z] = part_in_out[slot]

    every = list(range(GROUP - 1, -1, -1))

    def chain(value):
        turned = [value]
        for source in every[:-1]:
            turned.append(nt(turned[-1], transition(source)).astype(BF16))
        return turned

    def send_part_lone(which):
        return pltpu.make_async_remote_copy(
            src_ref=part_lone_out, dst_ref=part_lone.at[which, z],
            send_sem=pl_send, recv_sem=pl_recv.at[which, z],
            device_id={"ctx": 2 * GROUP}, device_id_type=MESH,
        )

    def lone_rows(hand_down):
        send_lone().wait_recv()
        turned = chain(lone_in[...])
        if hand_down:
            lone_out[...] = nt(turned[-1], transition(0)).astype(BF16)
            send_lone().start()
        mixed, log_sum = attend(turned, every, jnp.zeros((TILE, 1), F32))
        part_lone_out[0:TILE] = mixed
        part_lone_out[TILE:] = pieces(log_rows(log_sum))

    @pl.when(x == 1)
    def _():
        lone_rows(True)
        send_part_lone(0).start()

    def send_part_cross(slot):
        return pltpu.make_async_remote_copy(
            src_ref=part_cross_out.at[slot], dst_ref=part_cross.at[z],
            send_sem=pc_send.at[slot], recv_sem=pc_recv.at[z],
            device_id={"ctx": base + GROUP + slot}, device_id_type=MESH,
        )

    @pl.when(jnp.logical_not(is_odd))
    def _():
        def cross(slot, carry):
            send_forward(slot).wait_recv()

            def rows(tile, carry):
                at = pl.ds(pl.multiple_of(tile * TILE, TILE), TILE)
                docs = cross_in[slot, BLOCK:].astype(F32)
                docs = jnp.where(tile == 0, docs[0:2], docs[2:4])
                mixed, log_sum = attend(chain(cross_in[slot, at]), every, query_documents(docs, tile))
                part_cross_out[slot, at] = mixed
                log_ref[tile] = log_rows(log_sum)
                return carry

            lax.fori_loop(0, BLOCK // TILE, rows, 0)
            part_cross_out[slot, BLOCK:] = pieces(jnp.concatenate([log_ref[0], log_ref[1]], axis=0))
            send_part_cross(slot).start()
            return carry

        lax.fori_loop(0, GROUP, cross, 0)

    @pl.when(x == 0)
    def _():
        lone_rows(False)
        send_part_lone(1).start()

    def merge(head, part, count):
        logs = unpieced(part[count * SUB : count * SUB + 16], count)
        for a in range(count):
            at = slice(a * SUB, (a + 1) * SUB)
            log_sum = rows_to_column(logs[a : a + 1], eye)
            old = max_ref[head, at]
            new = jnp.maximum(old, log_sum)
            keep = jnp.exp2(old - new)
            add = jnp.exp2(log_sum - new)
            acc_ref[head, at] = acc_ref[head, at] * keep + part[at].astype(F32) * add
            sum_ref[head, at] = sum_ref[head, at] * keep + add
            max_ref[head, at] = new

    def part_in_arrival(head):
        return pltpu.make_async_remote_copy(
            src_ref=part_in_out.at[head], dst_ref=part_in.at[head],
            send_sem=pi_send.at[head], recv_sem=pi_recv.at[head],
            device_id={"ctx": base + head}, device_id_type=MESH,
        )

    def part_cross_arrival(head):
        return pltpu.make_async_remote_copy(
            src_ref=part_cross_out.at[head], dst_ref=part_cross.at[head],
            send_sem=pc_send.at[head], recv_sem=pc_recv.at[head],
            device_id={"ctx": base - GROUP + head}, device_id_type=MESH,
        )

    def part_lone_arrival(which, head):
        return pltpu.make_async_remote_copy(
            src_ref=part_lone_out, dst_ref=part_lone.at[which, head],
            send_sem=pl_send, recv_sem=pl_recv.at[which, head],
            device_id={"ctx": (1 - which) * GROUP + head}, device_id_type=MESH,
        )

    @pl.when(z > 0)
    def _():
        def body(head, carry):
            @pl.when(head != z)
            def _():
                part_in_arrival(head).wait_recv()

            merge(head, part_in[head], N_SUB)
            return carry

        lax.fori_loop(0, N_HEAD, body, 0)

    @pl.when((x == 2) & (z == 0))
    def _():
        def body(head, carry):
            for which in range(2):
                part_lone_arrival(which, head).wait_recv()
                merge(head, part_lone[which, head], 2)
            return carry

        lax.fori_loop(0, N_HEAD, body, 0)

    @pl.when(is_odd)
    def _():
        def body(head, carry):
            part_cross_arrival(head).wait_recv()
            merge(head, part_cross[head], N_SUB)
            return carry

        lax.fori_loop(0, N_HEAD, body, 0)

    for head in range(N_HEAD):
        out_ref[:, head * HEAD : (head + 1) * HEAD] = (acc_ref[head] / sum_ref[head]).astype(BF16)

    for slot in range(GROUP):
        @pl.when(slot != z)
        def _():
            send_packet(slot).wait_send()

        @pl.when(is_odd)
        def _():
            send_forward(slot).wait_send()

        @pl.when(jnp.logical_not(is_odd))
        def _():
            send_part_cross(slot).wait_send()

        if slot > 0:
            @pl.when(slot != z)
            def _():
                send_part_in(slot).wait_send()

    @pl.when((x == 1) | (x == 2))
    def _():
        send_lone().wait_send()

    @pl.when(x < 2)
    def _():
        send_part_lone(0).wait_send()


def attention(queries, keys, values, vectors, logits, docs):
    part = lambda *shape: pltpu.VMEM(shape, BF16)
    wide = lambda *shape: pltpu.VMEM(shape, F32)
    dma = lambda *shape: pltpu.SemaphoreType.DMA(shape)
    return pl.pallas_call(
        attention_kernel,
        out_shape=jax.ShapeDtypeStruct((BLOCK, N_HEAD * HEAD), BF16),
        in_specs=[pl.BlockSpec(memory_space=pltpu.VMEM)] * 6,
        out_specs=pl.BlockSpec(memory_space=pltpu.VMEM),
        scratch_shapes=[
            part(7, SUB, SUB), wide(BLOCK, N_HEAD), part(N_HEAD, PACKET, HEAD), part(GROUP, PACKET, HEAD),
            part(6, BLOCK, HEAD), part(GROUP, PART, HEAD), part(GROUP, PART, HEAD), part(TILE, HEAD), part(TILE, HEAD),
            part(GROUP, PART, HEAD), part(GROUP, PART, HEAD), part(PART_HALF, HEAD), part(N_HEAD, PART, HEAD),
            part(N_HEAD, PART, HEAD), part(2, N_HEAD, PART_HALF, HEAD), wide(2, 2, SUB),
            wide(N_HEAD, BLOCK, HEAD), wide(N_HEAD, BLOCK, HEAD), wide(N_HEAD, BLOCK, HEAD),
            pltpu.SemaphoreType.DMA, dma(GROUP), dma(GROUP), dma(GROUP), dma(GROUP),
            pltpu.SemaphoreType.DMA, pltpu.SemaphoreType.DMA,
            dma(GROUP), dma(GROUP), dma(GROUP), dma(GROUP), pltpu.SemaphoreType.DMA, dma(2, GROUP),
        ],
        compiler_params=pltpu.CompilerParams(
            collective_id=0, has_side_effects=True, vmem_limit_bytes=48 * 1024 * 1024
        ),
    )(queries, keys, values, vectors, logits, docs)


def on_device(queries, keys, values, vectors, logits, docs, out_weight):
    docs = docs.astype(F32).reshape(N_SUB, SUB)
    attended = attention(queries, keys, values, vectors, logits, docs)
    return lax.psum_scatter(
        jnp.dot(attended, out_weight, preferred_element_type=F32).astype(BF16),
        "head",
        scatter_dimension=0,
        tiled=True,
    )


def solution(mesh):
    return jax.shard_map(
        on_device,
        mesh=mesh,
        in_specs=(
            P("ctx", "head"),
            P("ctx", "head"),
            P("ctx", "head"),
            P("ctx", "head"),
            P("ctx", "head"),
            P("ctx"),
            P("head", None),
        ),
        out_specs=P(("ctx", "head"), None),
        check_vma=False,
    )
```

```python
import math

import jax
import jax.numpy as jnp
from jax import lax
from jax.experimental import pallas as pl
from jax.experimental.pallas import tpu as pltpu
from jax.sharding import PartitionSpec as P

MESH = pl.DeviceIdType.MESH
F32 = jnp.float32
BF16 = jnp.bfloat16

HEAD = 128
BLOCK = 512
SUB = 128
N_SUB = 4
N_HEAD = 4
GROUP = 4
TILE = 256
COLS = 512
N_COLS = 8
ROWS = 64
MODEL = 4096
NEG = -1e30
UNIT = math.log2(math.e) / math.sqrt(HEAD)

AT_Q, AT_K, AT_V, AT_T, AT_D = 0, 512, 1024, 1536, 1664
PACKET = 1680
PART = BLOCK + 16
PART_HALF = TILE + 16


def nn(a, b):
    return lax.dot_general(a, b, (((1,), (0,)), ((), ())), preferred_element_type=F32)


def nt(a, b):
    return lax.dot_general(a, b, (((1,), (1,)), ((), ())), preferred_element_type=F32)


def halves(a):
    high = a.astype(BF16)
    return high, (a - high.astype(F32)).astype(BF16)


def rows_to_column(row, eye):
    return jnp.sum(jnp.where(eye, row, 0.0), axis=1, keepdims=True)


def column_to_rows(column, eye):
    return jnp.sum(jnp.where(eye, column, 0.0), axis=0, keepdims=True)


def pieces(rows):
    high = rows.astype(BF16).astype(F32)
    rest = rows - high
    middle = rest.astype(BF16).astype(F32)
    low = rest - middle
    pad = jnp.zeros((16 - 3 * rows.shape[0], rows.shape[1]), F32)
    return jnp.concatenate([high, middle, low, pad], axis=0).astype(BF16)


def unpieced(tail, count):
    tail = tail.astype(F32)
    return tail[:count] + tail[count : 2 * count] + tail[2 * count : 3 * count]


def identity_masks():
    row = lax.broadcasted_iota(jnp.int32, (SUB, SUB), 0)
    col = lax.broadcasted_iota(jnp.int32, (SUB, SUB), 1)
    return row, col


def layer_kernel(
    q_hbm, k_hbm, v_hbm, u_hbm, logit_ref, doc_ref, w_hbm, out_ref,
    q_ref, k_ref, v_ref, u_ref, w_ref, level_ref, beta_ref, packet_out, packet_in, turned_ref, forward_ref, cross_in, lone_in, lone_out,
    part_in_out, part_cross_out, part_lone_out, part_in, part_cross, part_lone, log_ref,
    acc_ref, max_ref, sum_ref,
    att_ref, mine_ref, pair_out, pair_in, far_out, far_in, relay_out, relay_in, near_out, near_in,
    load_sem, w_sem, own_sem, pk_send, pk_recv, xf_send, xf_recv, lone_send, lone_recv,
    pi_send, pi_recv, pc_send, pc_recv, pl_send, pl_recv,
    pair_send, pair_recv, far_send, far_recv, relay_send, relay_recv, near_send, near_recv,
):
    me = lax.axis_index("ctx")
    n_ctx = lax.axis_size("ctx")
    x = me // GROUP
    z = lax.rem(me, GROUP)
    base = x * GROUP

    here = lax.axis_index("head")
    y = here // 2
    core = lax.rem(here, 2)

    barrier = pltpu.get_barrier_semaphore()
    others = [y * 2 + 1 - core] + [lax.rem(y + step, 4) * 2 + core for step in (1, 3)]
    for other in others:
        pl.semaphore_signal(barrier, inc=1, device_id={"head": other}, device_id_type=MESH)

    def greet(step, carry):
        pl.semaphore_signal(barrier, inc=1, device_id={"ctx": lax.rem(me + step, n_ctx)}, device_id_type=MESH)
        return carry

    lax.fori_loop(1, n_ctx, greet, 0)

    def load(index, head):
        source = (q_hbm, k_hbm, v_hbm, u_hbm)[index]
        target = (q_ref, k_ref, v_ref, u_ref)[index]
        lanes = pl.ds(pl.multiple_of(head * HEAD, HEAD), HEAD)
        return pltpu.make_async_copy(source.at[:, lanes], target.at[head], load_sem.at[index, head])

    def start_loads(turn, carry):
        for index in range(4):
            load(index, lax.rem(z + 1 + turn, N_HEAD)).start()
        return carry

    lax.fori_loop(0, N_HEAD, start_loads, 0)
    weight_load = pltpu.make_async_copy(w_hbm, w_ref, w_sem)
    weight_load.start()

    row, col = identity_masks()
    for level in range(7):
        hit = ((row >> level) + 1 == (col >> level)) & (((row >> level) & 1) == 0)
        level_ref[level] = jnp.where(hit, 1.0, 0.0).astype(BF16)
    beta_ref[...] = 2.0 * jax.nn.sigmoid(logit_ref[...])

    def send_packet(head):
        return pltpu.make_async_remote_copy(
            src_ref=packet_out.at[head], dst_ref=packet_in.at[z],
            send_sem=pk_send.at[head], recv_sem=pk_recv.at[z],
            device_id={"ctx": base + head}, device_id_type=MESH,
        )

    def head_step(turn, carry):
        head = lax.rem(z + 1 + turn, N_HEAD)
        row, col = identity_masks()
        eye = row == col
        upper = col > row
        lower = col < row
        causal = col <= row
        one = jnp.where(eye, 1.0, 0.0)
        for index in range(4):
            load(index, head).wait()
        beta = beta_ref[pl.ds(head, 1), :]
        subs = range(N_SUB)
        at = [slice(a * SUB, (a + 1) * SUB) for a in subs]
        q = [q_ref[head, at[a]] for a in subs]
        k = [k_ref[head, at[a]] for a in subs]
        v = [v_ref[head, at[a]] for a in subs]
        u = [u_ref[head, at[a]] for a in subs]
        tau, tau_row, lt, low_t, lt_low, skew_t, qk, skew, aq = [], [], [], [], [], [], [], [], []
        for a in subs:
            wide = u[a].astype(F32)
            tau.append(rows_to_column(beta[:, at[a]], eye) / (jnp.sum(wide * wide, axis=1, keepdims=True) + 1e-6))
            tau_row.append(column_to_rows(tau[a], eye))
            gram = jnp.where(upper, nt(u[a], u[a]) * tau[a], 0.0)
            high, low = halves(gram)
            lt.append(high)
            lt_low.append(low)
        inverse = []
        for a in subs:
            inverse.append((one - (lt[a] * level_ref[0]).astype(F32)).astype(BF16))
        for level in range(1, 7):
            first = [nn(inverse[a], lt[a] * level_ref[level]).astype(BF16) for a in subs]
            inverse = [
                (inverse[a].astype(F32) - nn(first[a], inverse[a])).astype(BF16) for a in subs
            ]
        residual = [
            (one - inverse[a].astype(F32) - (nn(lt[a], inverse[a]) + nn(lt_low[a], inverse[a]))).astype(BF16)
            for a in subs
        ]
        solved = [inverse[a].astype(F32) + nn(inverse[a], residual[a]) for a in subs]
        z_full, trans, keys, intra, turned = [], [], [], [], []
        for a in subs:
            high, low = halves(solved[a] * tau_row[a])
            z_full.append(nn(high, u[a]) + nn(low, u[a]))
        for a in subs:
            high, low = halves(z_full[a])
            across = u[a].astype(F32).T.astype(BF16)
            trans.append(one - (nn(across, high) + nn(across, low)))
            skew_t = jnp.where(upper, nt(k[a], u[a]), 0.0).astype(BF16)
            keys.append(k[a].astype(F32) - nn(skew_t, high))
        for a in subs:
            a_high, a_low = halves(jnp.where(causal, nt(q[a], u[a]), 0.0) * tau_row[a])
            s_high, s_low = halves(solved[a])
            y = (nt(a_high, s_high) + nt(a_low, s_high) + nt(a_high, s_low)).astype(BF16)
            skew = jnp.where(lower, nt(u[a], k[a]), 0.0).astype(BF16)
            intra.append((nt(q[a], k[a]) - nn(y, skew)) * UNIT)
            turned.append((q[a].astype(F32) - nn(y, u[a])) * UNIT)

        def as_b(value):
            return value.astype(BF16)

        t_b = [as_b(trans[a]) for a in subs]
        near_10 = nt(as_b(turned[1]), as_b(keys[0]))
        near_32 = nt(as_b(turned[3]), as_b(keys[2]))
        turned[1] = nt(as_b(turned[1]), t_b[0])
        turned[3] = nt(as_b(turned[3]), t_b[2])
        keys[0] = nn(as_b(keys[0]), t_b[1])
        keys[2] = nn(as_b(keys[2]), t_b[3])

        def product(left, right):
            left_high, left_low = halves(left)
            right_high, right_low = halves(right)
            return nn(left_high, right_high) + nn(left_low, right_high) + nn(left_high, right_low)

        pair_a = product(trans[0], trans[1])
        pair_b = product(trans[2], trans[3])
        late = jnp.concatenate([as_b(turned[2]), as_b(turned[3])], axis=0)
        early = jnp.concatenate([as_b(keys[0]), as_b(keys[1])], axis=0)
        far = nt(late, early)
        late = nt(late, as_b(pair_a))
        early = nn(early, as_b(pair_b))
        whole = product(pair_a, pair_b)
        packet_out[head, AT_Q : AT_Q + 256] = as_b(jnp.concatenate([turned[0], turned[1]], axis=0))
        packet_out[head, AT_Q + 256 : AT_Q + 512] = as_b(late)
        packet_out[head, AT_K : AT_K + 256] = as_b(early)
        packet_out[head, AT_K + 256 : AT_K + 512] = as_b(jnp.concatenate([keys[2], keys[3]], axis=0))
        packet_out[head, AT_V : AT_V + 512] = jnp.concatenate(v, axis=0)
        packet_out[head, AT_T : AT_T + 128] = as_b(whole)
        docs = doc_ref[...].astype(F32)
        packet_out[head, AT_D : AT_D + 16] = as_b(
            jnp.concatenate([docs, jnp.zeros((16 - N_SUB, SUB), F32)], axis=0)
        )

        @pl.when(turn == 0)
        def _():
            pl.semaphore_wait(barrier, n_ctx - 1 + len(others))

        @pl.when(turn < N_HEAD - 1)
        def _():
            send_packet(head).start()

        tiles = [
            [intra[0]],
            [near_10, intra[1]],
            [far[:SUB, :SUB], far[:SUB, SUB:], intra[2]],
            [far[SUB:, :SUB], far[SUB:, SUB:], near_32, intra[3]],
        ]
        for a in subs:
            mine = rows_to_column(docs[a : a + 1], eye)
            scores = []
            for b in range(a + 1):
                allowed = mine == docs[b : b + 1]
                if b == a:
                    allowed = allowed & causal
                scores.append(jnp.where(allowed, tiles[a][b], NEG))
            top = scores[0]
            for score in scores[1:]:
                top = jnp.maximum(top, score)
            top = jnp.max(top, axis=1, keepdims=True)
            weights = [jnp.exp2(score - top) for score in scores]
            total = weights[0]
            for weight in weights[1:]:
                total = total + weight
            total = jnp.sum(total, axis=1, keepdims=True)
            joined = jnp.concatenate([as_b(weight) for weight in weights], axis=1)
            acc_ref[head, at[a]] = nn(joined, jnp.concatenate(v[: a + 1], axis=0))
            max_ref[head, at[a]] = jnp.broadcast_to(top, (SUB, HEAD))
            sum_ref[head, at[a]] = jnp.broadcast_to(total, (SUB, HEAD))
        return carry

    lax.fori_loop(0, N_HEAD, head_step, 0)

    own = pltpu.make_async_copy(packet_out.at[z], packet_in.at[z], own_sem)
    own.start()
    own.wait()

    def packet_arrival(slot):
        return pltpu.make_async_remote_copy(
            src_ref=packet_out.at[slot], dst_ref=packet_in.at[slot],
            send_sem=pk_send.at[slot], recv_sem=pk_recv.at[slot],
            device_id={"ctx": base + slot}, device_id_type=MESH,
        )

    for slot in range(GROUP):
        @pl.when(slot != z)
        def _():
            packet_arrival(slot).wait_recv()

    def transition(slot):
        return packet_in[slot, AT_T : AT_T + 128]

    def send_forward(slot):
        return pltpu.make_async_remote_copy(
            src_ref=forward_ref.at[slot], dst_ref=cross_in.at[slot],
            send_sem=xf_send.at[slot], recv_sem=xf_recv.at[slot],
            device_id={"ctx": lax.rem(me + n_ctx - GROUP, n_ctx)}, device_id_type=MESH,
        )

    def send_lone():
        return pltpu.make_async_remote_copy(
            src_ref=lone_out, dst_ref=lone_in,
            send_sem=lone_send, recv_sem=lone_recv,
            device_id={"ctx": lax.rem(me + n_ctx - GROUP, n_ctx)}, device_id_type=MESH,
        )

    @pl.when(x == 2)
    def _():
        lone_out[...] = packet_in[0, AT_Q : AT_Q + TILE]
        send_lone().start()

    is_odd = lax.rem(x, 2) == 1
    for slot in range(GROUP):
        value = packet_in[slot, AT_Q : AT_Q + BLOCK]
        for source in range(slot - 1, -1, -1):
            turned_ref[slot * (slot - 1) // 2 + source] = value
            if source > 0:
                value = nt(value, transition(source)).astype(BF16)

        @pl.when(is_odd)
        def _():
            last = value if slot == 0 else nt(value, transition(0)).astype(BF16)
            forward_ref[slot, 0:BLOCK] = last
            forward_ref[slot, BLOCK:] = packet_in[slot, AT_D : AT_D + 16]
            send_forward(slot).start()

    row, col = identity_masks()
    eye = row == col

    def key_documents(slot):
        docs = packet_in[slot, AT_D : AT_D + 16].astype(F32)
        return [docs[a : a + 1] for a in range(N_SUB)]

    def attend(turned, slots, query_docs):
        scores = []
        for value, slot in zip(turned, slots):
            raw = nt(value, packet_in[slot, AT_K : AT_K + BLOCK])
            for a, docs in enumerate(key_documents(slot)):
                scores.append(jnp.where(query_docs == docs, raw[:, a * SUB : (a + 1) * SUB], NEG))
        top = scores[0]
        for score in scores[1:]:
            top = jnp.maximum(top, score)
        top = jnp.max(top, axis=1, keepdims=True)
        total = None
        mixed = None
        for index, slot in enumerate(slots):
            weights = [jnp.exp2(score - top) for score in scores[index * N_SUB : (index + 1) * N_SUB]]
            for weight in weights:
                total = weight if total is None else total + weight
            joined = jnp.concatenate([weight.astype(BF16) for weight in weights], axis=1)
            term = nn(joined, packet_in[slot, AT_V : AT_V + BLOCK])
            mixed = term if mixed is None else mixed + term
        total = jnp.sum(total, axis=1, keepdims=True)
        return (mixed / total).astype(BF16), top + jnp.log2(total)

    def query_documents(docs, tile):
        columns = [rows_to_column(docs[a : a + 1], eye) for a in range(2)]
        return jnp.concatenate(columns, axis=0)

    def log_rows(log_sum):
        return jnp.concatenate(
            [column_to_rows(log_sum[a * SUB : (a + 1) * SUB], eye) for a in range(2)], axis=0
        )

    def send_part_in(slot):
        return pltpu.make_async_remote_copy(
            src_ref=part_in_out.at[slot], dst_ref=part_in.at[z],
            send_sem=pi_send.at[slot], recv_sem=pi_recv.at[z],
            device_id={"ctx": base + slot}, device_id_type=MESH,
        )

    for slot in range(1, GROUP):
        docs = packet_in[slot, AT_D : AT_D + 16].astype(F32)
        logs = []
        for tile in range(BLOCK // TILE):
            at = slice(tile * TILE, (tile + 1) * TILE)
            sources = list(range(slot - 1, -1, -1))
            turned = [turned_ref[slot * (slot - 1) // 2 + source, at] for source in sources]
            mixed, log_sum = attend(turned, sources, query_documents(docs[2 * tile : 2 * tile + 2], tile))
            part_in_out[slot, at] = mixed
            logs.append(log_rows(log_sum))
        part_in_out[slot, BLOCK:] = pieces(jnp.concatenate(logs, axis=0))

        @pl.when(slot != z)
        def _():
            send_part_in(slot).start()

        @pl.when(slot == z)
        def _():
            part_in[z] = part_in_out[slot]

    every = list(range(GROUP - 1, -1, -1))

    def chain(value):
        turned = [value]
        for source in every[:-1]:
            turned.append(nt(turned[-1], transition(source)).astype(BF16))
        return turned

    def send_part_lone(which):
        return pltpu.make_async_remote_copy(
            src_ref=part_lone_out, dst_ref=part_lone.at[which, z],
            send_sem=pl_send, recv_sem=pl_recv.at[which, z],
            device_id={"ctx": 2 * GROUP}, device_id_type=MESH,
        )

    def lone_rows(hand_down):
        send_lone().wait_recv()
        turned = chain(lone_in[...])
        if hand_down:
            lone_out[...] = nt(turned[-1], transition(0)).astype(BF16)
            send_lone().start()
        mixed, log_sum = attend(turned, every, jnp.zeros((TILE, 1), F32))
        part_lone_out[0:TILE] = mixed
        part_lone_out[TILE:] = pieces(log_rows(log_sum))

    @pl.when(x == 1)
    def _():
        lone_rows(True)
        send_part_lone(0).start()

    def send_part_cross(slot):
        return pltpu.make_async_remote_copy(
            src_ref=part_cross_out.at[slot], dst_ref=part_cross.at[z],
            send_sem=pc_send.at[slot], recv_sem=pc_recv.at[z],
            device_id={"ctx": base + GROUP + slot}, device_id_type=MESH,
        )

    @pl.when(jnp.logical_not(is_odd))
    def _():
        def cross(slot, carry):
            send_forward(slot).wait_recv()

            def rows(tile, carry):
                at = pl.ds(pl.multiple_of(tile * TILE, TILE), TILE)
                docs = cross_in[slot, BLOCK:].astype(F32)
                docs = jnp.where(tile == 0, docs[0:2], docs[2:4])
                mixed, log_sum = attend(chain(cross_in[slot, at]), every, query_documents(docs, tile))
                part_cross_out[slot, at] = mixed
                log_ref[tile] = log_rows(log_sum)
                return carry

            lax.fori_loop(0, BLOCK // TILE, rows, 0)
            part_cross_out[slot, BLOCK:] = pieces(jnp.concatenate([log_ref[0], log_ref[1]], axis=0))
            send_part_cross(slot).start()
            return carry

        lax.fori_loop(0, GROUP, cross, 0)

    @pl.when(x == 0)
    def _():
        lone_rows(False)
        send_part_lone(1).start()

    def merge(head, part, count):
        logs = unpieced(part[count * SUB : count * SUB + 16], count)
        for a in range(count):
            at = slice(a * SUB, (a + 1) * SUB)
            log_sum = rows_to_column(logs[a : a + 1], eye)
            old = max_ref[head, at]
            new = jnp.maximum(old, log_sum)
            keep = jnp.exp2(old - new)
            add = jnp.exp2(log_sum - new)
            acc_ref[head, at] = acc_ref[head, at] * keep + part[at].astype(F32) * add
            sum_ref[head, at] = sum_ref[head, at] * keep + add
            max_ref[head, at] = new

    def part_in_arrival(head):
        return pltpu.make_async_remote_copy(
            src_ref=part_in_out.at[head], dst_ref=part_in.at[head],
            send_sem=pi_send.at[head], recv_sem=pi_recv.at[head],
            device_id={"ctx": base + head}, device_id_type=MESH,
        )

    def part_cross_arrival(head):
        return pltpu.make_async_remote_copy(
            src_ref=part_cross_out.at[head], dst_ref=part_cross.at[head],
            send_sem=pc_send.at[head], recv_sem=pc_recv.at[head],
            device_id={"ctx": base - GROUP + head}, device_id_type=MESH,
        )

    def part_lone_arrival(which, head):
        return pltpu.make_async_remote_copy(
            src_ref=part_lone_out, dst_ref=part_lone.at[which, head],
            send_sem=pl_send, recv_sem=pl_recv.at[which, head],
            device_id={"ctx": (1 - which) * GROUP + head}, device_id_type=MESH,
        )

    @pl.when(z > 0)
    def _():
        def body(head, carry):
            @pl.when(head != z)
            def _():
                part_in_arrival(head).wait_recv()

            merge(head, part_in[head], N_SUB)
            return carry

        lax.fori_loop(0, N_HEAD, body, 0)

    @pl.when((x == 2) & (z == 0))
    def _():
        def body(head, carry):
            for which in range(2):
                part_lone_arrival(which, head).wait_recv()
                merge(head, part_lone[which, head], 2)
            return carry

        lax.fori_loop(0, N_HEAD, body, 0)

    @pl.when(is_odd)
    def _():
        def body(head, carry):
            part_cross_arrival(head).wait_recv()
            merge(head, part_cross[head], N_SUB)
            return carry

        lax.fori_loop(0, N_HEAD, body, 0)

    for side in range(2):
        for place, step in enumerate((2, 1, 3, 0)):
            owner = lax.rem(y + step, 4) * 2 + (1 - core if side == 0 else core)
            rows = pl.ds(pl.multiple_of(owner * ROWS, ROWS), ROWS)
            for head in range(N_HEAD):
                att_ref[side, place * ROWS : (place + 1) * ROWS, head * HEAD : (head + 1) * HEAD] = (
                    acc_ref[head, rows] / sum_ref[head, rows]
                ).astype(BF16)
    weight_load.wait()

    def sided(t):
        sign = 1 - 2 * lax.rem(t, 2)
        onward = lax.rem(y + sign + 4, 4) * 2 + core
        back = lax.rem(y - sign + 4, 4) * 2 + core
        return onward, back

    def columns(t):
        return pl.ds(pl.multiple_of((t // 2) * COLS + lax.rem(t, 2) * (MODEL // 2), COLS), COLS)

    def remote(source, target, send_sem, recv_sem, t, other):
        return pltpu.make_async_remote_copy(
            src_ref=source.at[t], dst_ref=target.at[t], send_sem=send_sem.at[t], recv_sem=recv_sem.at[t],
            device_id={"head": other}, device_id_type=MESH,
        )

    def send_pair(t):
        return remote(pair_out, pair_in, pair_send, pair_recv, t, others[0])

    def send_far(t):
        return remote(far_out, far_in, far_send, far_recv, t, sided(t)[0])

    def send_relay(t):
        return remote(relay_out, relay_in, relay_send, relay_recv, t, sided(t)[0])

    def send_near(t):
        return remote(near_out, near_in, near_send, near_recv, t, sided(t)[1])

    def project(t, carry):
        @pl.when(t < N_COLS)
        def _():
            weights = w_ref[:, columns(t)]
            pair_out[t] = nn(att_ref[0], weights).astype(BF16)
            send_pair(t).start()
            mine_ref[t] = nn(att_ref[1], weights)

        @pl.when((t >= 1) & (t < N_COLS + 1))
        def _():
            p = t - 1
            send_pair(p).wait_recv()
            both = mine_ref[p] + pair_in[p].astype(F32)
            up = lax.rem(p, 2) == 0
            one, two = both[ROWS : 2 * ROWS], both[2 * ROWS : 3 * ROWS]
            far_out[p] = both[0:ROWS].astype(BF16)
            send_far(p).start()
            near_out[p] = jnp.where(up, two, one).astype(BF16)
            send_near(p).start()
            mine_ref[p, 0:ROWS] = jnp.where(up, one, two)
            mine_ref[p, 3 * ROWS :] = both[3 * ROWS :]

        @pl.when(t >= 3)
        def _():
            p = t - 3
            send_far(p).wait_recv()
            relay_out[p] = (mine_ref[p, 0:ROWS] + far_in[p].astype(F32)).astype(BF16)
            send_relay(p).start()

        return carry

    lax.fori_loop(0, N_COLS + 3, project, 0)

    def finish(t, carry):
        send_near(t).wait_recv()
        send_relay(t).wait_recv()
        total = mine_ref[t, 3 * ROWS :] + near_in[t].astype(F32) + relay_in[t].astype(F32)
        out_ref[:, columns(t)] = total.astype(BF16)
        send_pair(t).wait_send()
        send_far(t).wait_send()
        send_near(t).wait_send()
        send_relay(t).wait_send()
        return carry

    lax.fori_loop(0, N_COLS, finish, 0)

    for slot in range(GROUP):
        @pl.when(slot != z)
        def _():
            send_packet(slot).wait_send()

        @pl.when(is_odd)
        def _():
            send_forward(slot).wait_send()

        @pl.when(jnp.logical_not(is_odd))
        def _():
            send_part_cross(slot).wait_send()

        if slot > 0:
            @pl.when(slot != z)
            def _():
                send_part_in(slot).wait_send()

    @pl.when((x == 1) | (x == 2))
    def _():
        send_lone().wait_send()

    @pl.when(x < 2)
    def _():
        send_part_lone(0).wait_send()


def layer(queries, keys, values, vectors, logits, docs, out_weight):
    part = lambda *shape: pltpu.VMEM(shape, BF16)
    wide = lambda *shape: pltpu.VMEM(shape, F32)
    dma = lambda *shape: pltpu.SemaphoreType.DMA(shape)
    return pl.pallas_call(
        layer_kernel,
        out_shape=jax.ShapeDtypeStruct((ROWS, MODEL), BF16),
        in_specs=[pl.BlockSpec(memory_space=pl.ANY)] * 4
        + [pl.BlockSpec(memory_space=pltpu.VMEM)] * 2
        + [pl.BlockSpec(memory_space=pl.ANY)],
        out_specs=pl.BlockSpec(memory_space=pltpu.VMEM),
        scratch_shapes=[
            *[part(N_HEAD, BLOCK, HEAD)] * 4, part(BLOCK, MODEL),
            part(7, SUB, SUB), wide(N_HEAD, BLOCK), part(N_HEAD, PACKET, HEAD), part(GROUP, PACKET, HEAD),
            part(6, BLOCK, HEAD), part(GROUP, PART, HEAD), part(GROUP, PART, HEAD), part(TILE, HEAD), part(TILE, HEAD),
            part(GROUP, PART, HEAD), part(GROUP, PART, HEAD), part(PART_HALF, HEAD), part(N_HEAD, PART, HEAD),
            part(N_HEAD, PART, HEAD), part(2, N_HEAD, PART_HALF, HEAD), wide(2, 2, SUB),
            wide(N_HEAD, BLOCK, HEAD), wide(N_HEAD, BLOCK, HEAD), wide(N_HEAD, BLOCK, HEAD),
            part(2, TILE, BLOCK), wide(N_COLS, TILE, COLS), part(N_COLS, TILE, COLS), part(N_COLS, TILE, COLS),
            *[part(N_COLS, ROWS, COLS)] * 6,
            dma(4, N_HEAD), pltpu.SemaphoreType.DMA,
            pltpu.SemaphoreType.DMA, dma(GROUP), dma(GROUP), dma(GROUP), dma(GROUP),
            pltpu.SemaphoreType.DMA, pltpu.SemaphoreType.DMA,
            dma(GROUP), dma(GROUP), dma(GROUP), dma(GROUP), pltpu.SemaphoreType.DMA, dma(2, GROUP),
            *[dma(N_COLS)] * 8,
        ],
        compiler_params=pltpu.CompilerParams(
            collective_id=0, has_side_effects=True, vmem_limit_bytes=60 * 1024 * 1024
        ),
    )(queries, keys, values, vectors, logits, docs, out_weight)


def on_device(queries, keys, values, vectors, logits, docs, out_weight):
    return layer(queries, keys, values, vectors, logits.T, docs.reshape(N_SUB, SUB), out_weight)


def solution(mesh):
    return jax.shard_map(
        on_device,
        mesh=mesh,
        in_specs=(
            P("ctx", "head"),
            P("ctx", "head"),
            P("ctx", "head"),
            P("ctx", "head"),
            P("ctx", "head"),
            P("ctx"),
            P("head", None),
        ),
        out_specs=P(("ctx", "head"), None),
        check_vma=False,
    )
```

```python
import math

import jax
import jax.numpy as jnp
from jax import lax
from jax.experimental import pallas as pl
from jax.experimental.pallas import tpu as pltpu
from jax.sharding import PartitionSpec as P

MESH = pl.DeviceIdType.MESH
F32 = jnp.float32
BF16 = jnp.bfloat16

HEAD = 128
BLOCK = 512
SUB = 128
N_SUB = 4
N_HEAD = 4
GROUP = 4
TILE = 256
COLS = 512
N_COLS = 8
ROWS = 64
MODEL = 4096
NEG = -1e30
TRIANGLE = (0, 1, 3, 6)
UNIT = math.log2(math.e) / math.sqrt(HEAD)

TOGETHER = 2
AT_Q, AT_T, AT_D = 0, 512, 640
PACKET = 656
PART = BLOCK + 16
PART_HALF = TILE + 16


def nn(a, b):
    return lax.dot_general(a, b, (((1,), (0,)), ((), ())), preferred_element_type=F32)


def nt(a, b):
    return lax.dot_general(a, b, (((1,), (1,)), ((), ())), preferred_element_type=F32)


def halves(a):
    high = a.astype(BF16)
    return high, (a - high.astype(F32)).astype(BF16)


def rows_to_column(row, eye):
    return jnp.sum(jnp.where(eye, row, 0.0), axis=1, keepdims=True)


def column_to_rows(column, eye):
    return jnp.sum(jnp.where(eye, column, 0.0), axis=0, keepdims=True)


def pieces(rows):
    high = rows.astype(BF16).astype(F32)
    rest = rows - high
    middle = rest.astype(BF16).astype(F32)
    low = rest - middle
    pad = jnp.zeros((16 - 3 * rows.shape[0], rows.shape[1]), F32)
    return jnp.concatenate([high, middle, low, pad], axis=0).astype(BF16)


def unpieced(tail, count):
    tail = tail.astype(F32)
    return tail[:count] + tail[count : 2 * count] + tail[2 * count : 3 * count]


def identity_masks():
    row = lax.broadcasted_iota(jnp.int32, (SUB, SUB), 0)
    col = lax.broadcasted_iota(jnp.int32, (SUB, SUB), 1)
    return row, col


def layer_kernel(
    q_hbm, k_hbm, v_hbm, u_hbm, logit_ref, doc_ref, w_hbm, out_ref,
    q_ref, k_ref, v_ref, u_ref, w_ref, level_ref, beta_ref, packet_out, packet_in, keys_out, keys_in, values_in, score_ref, turned_ref, forward_ref, cross_in, lone_in, lone_out,
    part_in_out, part_cross_out, part_lone_out, part_in, part_cross, part_lone, log_ref,
    acc_ref, max_ref, sum_ref,
    att_ref, mine_ref, pair_out, pair_in, far_out, far_in, relay_out, relay_in, near_out, near_in,
    load_sem, w_sem, own_sem, pk_send, pk_recv, ks_send, ks_recv, vs_send, vs_recv, xf_send, xf_recv, lone_send, lone_recv,
    pi_send, pi_recv, pc_send, pc_recv, pl_send, pl_recv,
    pair_send, pair_recv, far_send, far_recv, relay_send, relay_recv, near_send, near_recv,
):
    me = lax.axis_index("ctx")
    n_ctx = lax.axis_size("ctx")
    x = me // GROUP
    z = lax.rem(me, GROUP)
    base = x * GROUP

    here = lax.axis_index("head")
    y = here // 2
    core = lax.rem(here, 2)

    barrier = pltpu.get_barrier_semaphore()
    others = [y * 2 + 1 - core] + [lax.rem(y + step, 4) * 2 + core for step in (1, 3)]
    for other in others:
        pl.semaphore_signal(barrier, inc=1, device_id={"head": other}, device_id_type=MESH)

    def greet(step, carry):
        pl.semaphore_signal(barrier, inc=1, device_id={"ctx": lax.rem(me + step, n_ctx)}, device_id_type=MESH)
        return carry

    lax.fori_loop(1, n_ctx, greet, 0)

    def load(index, head):
        source = (q_hbm, k_hbm, v_hbm, u_hbm)[index]
        target = (q_ref, k_ref, v_ref, u_ref)[index]
        lanes = pl.ds(pl.multiple_of(head * HEAD, HEAD), HEAD)
        return pltpu.make_async_copy(source.at[:, lanes], target.at[head], load_sem.at[index, head])

    def start_loads(turn, carry):
        for index in range(4):
            load(index, lax.rem(z + 1 + turn, N_HEAD)).start()
        return carry

    lax.fori_loop(0, N_HEAD, start_loads, 0)
    weight_load = pltpu.make_async_copy(w_hbm, w_ref, w_sem)
    weight_load.start()

    row, col = identity_masks()
    for level in range(7):
        hit = ((row >> level) + 1 == (col >> level)) & (((row >> level) & 1) == 0)
        level_ref[level] = jnp.where(hit, 1.0, 0.0).astype(BF16)
    beta_ref[...] = 2.0 * jax.nn.sigmoid(logit_ref[...])

    def to_group(source, target, send_sem, recv_sem, head, slot):
        return pltpu.make_async_remote_copy(
            src_ref=source.at[head], dst_ref=target.at[slot],
            send_sem=send_sem.at[head], recv_sem=recv_sem.at[slot],
            device_id={"ctx": base + head}, device_id_type=MESH,
        )

    def send_packet(head, slot):
        return to_group(packet_out, packet_in, pk_send, pk_recv, head, slot)

    def send_keys(head, slot):
        return to_group(keys_out, keys_in, ks_send, ks_recv, head, slot)

    def send_values(head, slot):
        return to_group(v_ref, values_in, vs_send, vs_recv, head, slot)

    def wait_value_load(turn, carry):
        load(2, lax.rem(z + 1 + turn, N_HEAD)).wait()
        return carry

    lax.fori_loop(0, N_HEAD, wait_value_load, 0)
    own_values = pltpu.make_async_copy(v_ref.at[z], values_in.at[z], own_sem.at[0])
    own_values.start()
    pl.semaphore_wait(barrier, n_ctx - 1 + len(others))

    def start_values(turn, carry):
        send_values(lax.rem(z + 1 + turn, N_HEAD), z).start()
        return carry

    lax.fori_loop(0, N_HEAD - 1, start_values, 0)

    def as_b(value):
        return value.astype(BF16)

    def product(left, right):
        left_high, left_low = halves(left)
        right_high, right_low = halves(right)
        return nn(left_high, right_high) + nn(left_low, right_high) + nn(left_high, right_low)

    def head_step(turn, carry):
        heads = [lax.rem(z + 1 + turn * TOGETHER + i, N_HEAD) for i in range(TOGETHER)]
        row, col = identity_masks()
        eye = row == col
        upper = col > row
        lower = col < row
        causal = col <= row
        one = jnp.where(eye, 1.0, 0.0)
        for head in heads:
            for index in (0, 1, 3):
                load(index, head).wait()
        subs = range(N_SUB * TOGETHER)
        at = [slice(a * SUB, (a + 1) * SUB) for a in range(N_SUB)]
        each = [(head, at[a]) for head in heads for a in range(N_SUB)]
        betas = [beta_ref[pl.ds(head, 1), :] for head in heads]
        beta = [row[:, rows] for row in betas for rows in at]
        q = [q_ref[head, rows] for head, rows in each]
        k = [k_ref[head, rows] for head, rows in each]
        u = [u_ref[head, rows] for head, rows in each]
        tau_row, lt, lt_low = [], [], []
        for a in subs:
            wide = u[a].astype(F32)
            tau = rows_to_column(beta[a], eye) / (jnp.sum(wide * wide, axis=1, keepdims=True) + 1e-6)
            tau_row.append(column_to_rows(tau, eye))
            gram = jnp.where(upper, nt(u[a], u[a]) * tau, 0.0)
            high, low = halves(gram)
            lt.append(high)
            lt_low.append(low)
        inverse = []
        for a in subs:
            inverse.append((one - (lt[a] * level_ref[0]).astype(F32)).astype(BF16))
        for level in range(1, 7):
            first = [nn(inverse[a], lt[a] * level_ref[level]).astype(BF16) for a in subs]
            inverse = [
                (inverse[a].astype(F32) - nn(first[a], inverse[a])).astype(BF16) for a in subs
            ]
        residual = [
            (one - inverse[a].astype(F32) - (nn(lt[a], inverse[a]) + nn(lt_low[a], inverse[a]))).astype(BF16)
            for a in subs
        ]
        solved = [inverse[a].astype(F32) + nn(inverse[a], residual[a]) for a in subs]
        z_full, trans, keys, intra, turned = [], [], [], [], []
        for a in subs:
            high, low = halves(solved[a] * tau_row[a])
            z_full.append(nn(high, u[a]) + nn(low, u[a]))
        for a in subs:
            high, low = halves(z_full[a])
            across = u[a].astype(F32).T.astype(BF16)
            trans.append(one - (nn(across, high) + nn(across, low)))
            skew_t = jnp.where(upper, nt(k[a], u[a]), 0.0).astype(BF16)
            keys.append(k[a].astype(F32) - nn(skew_t, high))
        for a in subs:
            a_high, a_low = halves(jnp.where(causal, nt(q[a], u[a]), 0.0) * tau_row[a])
            s_high, s_low = halves(solved[a])
            y = (nt(a_high, s_high) + nt(a_low, s_high) + nt(a_high, s_low)).astype(BF16)
            skew = jnp.where(lower, nt(u[a], k[a]), 0.0).astype(BF16)
            intra.append((nt(q[a], k[a]) - nn(y, skew)) * UNIT)
            turned.append((q[a].astype(F32) - nn(y, u[a])) * UNIT)

        t_b = [as_b(trans[a]) for a in subs]
        starts = range(0, N_SUB * TOGETHER, N_SUB)
        near, late, early, far = {}, {}, {}, {}
        for c in starts:
            for a in (c, c + 2):
                near[a] = nt(as_b(turned[a + 1]), as_b(keys[a]))
                turned[a + 1] = nt(as_b(turned[a + 1]), t_b[a])
                keys[a] = nn(as_b(keys[a]), t_b[a + 1])
        pair = {a: product(trans[a], trans[a + 1]) for c in starts for a in (c, c + 2)}
        for c in starts:
            late[c] = jnp.concatenate([as_b(turned[c + 2]), as_b(turned[c + 3])], axis=0)
            early[c] = jnp.concatenate([as_b(keys[c]), as_b(keys[c + 1])], axis=0)
        for c in starts:
            far[c] = nt(late[c], early[c])
            late[c] = nt(late[c], as_b(pair[c]))
            early[c] = nn(early[c], as_b(pair[c + 2]))
        docs = doc_ref[...].astype(F32)
        docs_tail = as_b(jnp.concatenate([docs, jnp.zeros((16 - N_SUB, SUB), F32)], axis=0))
        for head, c in zip(heads, starts):
            whole = product(pair[c], pair[c + 2])
            packet_out[head, AT_Q : AT_Q + 256] = as_b(jnp.concatenate([turned[c], turned[c + 1]], axis=0))
            packet_out[head, AT_Q + 256 : AT_Q + 512] = as_b(late[c])
            packet_out[head, AT_T : AT_T + 128] = as_b(whole)
            packet_out[head, AT_D : AT_D + 16] = docs_tail
            keys_out[head, 0:256] = as_b(early[c])
            keys_out[head, 256:512] = as_b(jnp.concatenate([keys[c + 2], keys[c + 3]], axis=0))

            @pl.when(head != z)
            def _():
                send_packet(head, z).start()

        for head, c in zip(heads, starts):
            for a in range(N_SUB):
                score_ref[head, TRIANGLE[a] + a] = intra[c + a]
            score_ref[head, 1] = near[c]
            score_ref[head, 8] = near[c + 2]
            for a in (2, 3):
                for b in (0, 1):
                    score_ref[head, TRIANGLE[a] + b] = far[c][(a - 2) * SUB : (a - 1) * SUB, b * SUB : (b + 1) * SUB]
        return carry

    lax.fori_loop(0, N_HEAD // TOGETHER, head_step, 0)

    own_packet = pltpu.make_async_copy(packet_out.at[z], packet_in.at[z], own_sem.at[1])
    own_packet.start()
    own_keys = pltpu.make_async_copy(keys_out.at[z], keys_in.at[z], own_sem.at[2])
    own_keys.start()

    def start_keys(turn, carry):
        send_keys(lax.rem(z + 1 + turn, N_HEAD), z).start()
        return carry

    lax.fori_loop(0, N_HEAD - 1, start_keys, 0)

    def own_attention(head, carry):
        row, col = identity_masks()
        eye = row == col
        causal = col <= row
        docs = doc_ref[...].astype(F32)
        for a in range(N_SUB):
            rows = slice(a * SUB, (a + 1) * SUB)
            mine = rows_to_column(docs[a : a + 1], eye)
            scores = []
            for b in range(a + 1):
                allowed = mine == docs[b : b + 1]
                if b == a:
                    allowed = allowed & causal
                scores.append(jnp.where(allowed, score_ref[head, TRIANGLE[a] + b], NEG))
            top = scores[0]
            for score in scores[1:]:
                top = jnp.maximum(top, score)
            top = jnp.max(top, axis=1, keepdims=True)
            weights = [jnp.exp2(score - top) for score in scores]
            total = weights[0]
            for weight in weights[1:]:
                total = total + weight
            total = jnp.sum(total, axis=1, keepdims=True)
            joined = jnp.concatenate([as_b(weight) for weight in weights], axis=1)
            acc_ref[head, rows] = nn(joined, v_ref[head, 0 : (a + 1) * SUB])
            max_ref[head, rows] = jnp.broadcast_to(top, (SUB, HEAD))
            sum_ref[head, rows] = jnp.broadcast_to(total, (SUB, HEAD))
        return carry

    lax.fori_loop(0, N_HEAD, own_attention, 0)

    own_packet.wait()
    for slot in range(GROUP):
        @pl.when(slot != z)
        def _():
            send_packet(slot, slot).wait_recv()

    def transition(slot):
        return packet_in[slot, AT_T : AT_T + 128]

    def send_forward(slot):
        return pltpu.make_async_remote_copy(
            src_ref=forward_ref.at[slot], dst_ref=cross_in.at[slot],
            send_sem=xf_send.at[slot], recv_sem=xf_recv.at[slot],
            device_id={"ctx": lax.rem(me + n_ctx - GROUP, n_ctx)}, device_id_type=MESH,
        )

    def send_lone():
        return pltpu.make_async_remote_copy(
            src_ref=lone_out, dst_ref=lone_in,
            send_sem=lone_send, recv_sem=lone_recv,
            device_id={"ctx": lax.rem(me + n_ctx - GROUP, n_ctx)}, device_id_type=MESH,
        )

    @pl.when(x == 2)
    def _():
        lone_out[...] = packet_in[0, AT_Q : AT_Q + TILE]
        send_lone().start()

    is_odd = lax.rem(x, 2) == 1
    for slot in range(GROUP):
        value = packet_in[slot, AT_Q : AT_Q + BLOCK]
        for source in range(slot - 1, -1, -1):
            turned_ref[slot * (slot - 1) // 2 + source] = value
            if source > 0:
                value = nt(value, transition(source)).astype(BF16)

        @pl.when(is_odd)
        def _():
            last = value if slot == 0 else nt(value, transition(0)).astype(BF16)
            forward_ref[slot, 0:BLOCK] = last
            forward_ref[slot, BLOCK:] = packet_in[slot, AT_D : AT_D + 16]
            send_forward(slot).start()

    row, col = identity_masks()
    eye = row == col

    own_values.wait()
    own_keys.wait()
    for slot in range(GROUP):
        @pl.when(slot != z)
        def _():
            send_values(slot, slot).wait_recv()
            send_keys(slot, slot).wait_recv()

    def key_documents(slot):
        docs = packet_in[slot, AT_D : AT_D + 16].astype(F32)
        return [docs[a : a + 1] for a in range(N_SUB)]

    def attend(turned, slots, query_docs):
        scores = []
        for value, slot in zip(turned, slots):
            raw = nt(value, keys_in[slot])
            for a, docs in enumerate(key_documents(slot)):
                scores.append(jnp.where(query_docs == docs, raw[:, a * SUB : (a + 1) * SUB], NEG))
        top = scores[0]
        for score in scores[1:]:
            top = jnp.maximum(top, score)
        top = jnp.max(top, axis=1, keepdims=True)
        total = None
        mixed = None
        for index, slot in enumerate(slots):
            weights = [jnp.exp2(score - top) for score in scores[index * N_SUB : (index + 1) * N_SUB]]
            for weight in weights:
                total = weight if total is None else total + weight
            joined = jnp.concatenate([weight.astype(BF16) for weight in weights], axis=1)
            term = nn(joined, values_in[slot])
            mixed = term if mixed is None else mixed + term
        total = jnp.sum(total, axis=1, keepdims=True)
        return (mixed / total).astype(BF16), top + jnp.log2(total)

    def query_documents(docs, tile):
        columns = [rows_to_column(docs[a : a + 1], eye) for a in range(2)]
        return jnp.concatenate(columns, axis=0)

    def log_rows(log_sum):
        return jnp.concatenate(
            [column_to_rows(log_sum[a * SUB : (a + 1) * SUB], eye) for a in range(2)], axis=0
        )

    def send_part_in(slot):
        return pltpu.make_async_remote_copy(
            src_ref=part_in_out.at[slot], dst_ref=part_in.at[z],
            send_sem=pi_send.at[slot], recv_sem=pi_recv.at[z],
            device_id={"ctx": base + slot}, device_id_type=MESH,
        )

    for slot in range(1, GROUP):
        docs = packet_in[slot, AT_D : AT_D + 16].astype(F32)
        logs = []
        for tile in range(BLOCK // TILE):
            at = slice(tile * TILE, (tile + 1) * TILE)
            sources = list(range(slot - 1, -1, -1))
            turned = [turned_ref[slot * (slot - 1) // 2 + source, at] for source in sources]
            mixed, log_sum = attend(turned, sources, query_documents(docs[2 * tile : 2 * tile + 2], tile))
            part_in_out[slot, at] = mixed
            logs.append(log_rows(log_sum))
        part_in_out[slot, BLOCK:] = pieces(jnp.concatenate(logs, axis=0))

        @pl.when(slot != z)
        def _():
            send_part_in(slot).start()

        @pl.when(slot == z)
        def _():
            part_in[z] = part_in_out[slot]

    every = list(range(GROUP - 1, -1, -1))

    def chain(value):
        turned = [value]
        for source in every[:-1]:
            turned.append(nt(turned[-1], transition(source)).astype(BF16))
        return turned

    def send_part_lone(which):
        return pltpu.make_async_remote_copy(
            src_ref=part_lone_out, dst_ref=part_lone.at[which, z],
            send_sem=pl_send, recv_sem=pl_recv.at[which, z],
            device_id={"ctx": 2 * GROUP}, device_id_type=MESH,
        )

    def lone_rows(hand_down):
        send_lone().wait_recv()
        turned = chain(lone_in[...])
        if hand_down:
            lone_out[...] = nt(turned[-1], transition(0)).astype(BF16)
            send_lone().start()
        mixed, log_sum = attend(turned, every, jnp.zeros((TILE, 1), F32))
        part_lone_out[0:TILE] = mixed
        part_lone_out[TILE:] = pieces(log_rows(log_sum))

    @pl.when(x == 1)
    def _():
        lone_rows(True)
        send_part_lone(0).start()

    def send_part_cross(slot):
        return pltpu.make_async_remote_copy(
            src_ref=part_cross_out.at[slot], dst_ref=part_cross.at[z],
            send_sem=pc_send.at[slot], recv_sem=pc_recv.at[z],
            device_id={"ctx": base + GROUP + slot}, device_id_type=MESH,
        )

    @pl.when(jnp.logical_not(is_odd))
    def _():
        def cross(slot, carry):
            send_forward(slot).wait_recv()

            def rows(tile, carry):
                at = pl.ds(pl.multiple_of(tile * TILE, TILE), TILE)
                docs = cross_in[slot, BLOCK:].astype(F32)
                docs = jnp.where(tile == 0, docs[0:2], docs[2:4])
                mixed, log_sum = attend(chain(cross_in[slot, at]), every, query_documents(docs, tile))
                part_cross_out[slot, at] = mixed
                log_ref[tile] = log_rows(log_sum)
                return carry

            lax.fori_loop(0, BLOCK // TILE, rows, 0)
            part_cross_out[slot, BLOCK:] = pieces(jnp.concatenate([log_ref[0], log_ref[1]], axis=0))
            send_part_cross(slot).start()
            return carry

        lax.fori_loop(0, GROUP, cross, 0)

    @pl.when(x == 0)
    def _():
        lone_rows(False)
        send_part_lone(1).start()

    def merge(head, part, count):
        logs = unpieced(part[count * SUB : count * SUB + 16], count)
        for a in range(count):
            at = slice(a * SUB, (a + 1) * SUB)
            log_sum = rows_to_column(logs[a : a + 1], eye)
            old = max_ref[head, at]
            new = jnp.maximum(old, log_sum)
            keep = jnp.exp2(old - new)
            add = jnp.exp2(log_sum - new)
            acc_ref[head, at] = acc_ref[head, at] * keep + part[at].astype(F32) * add
            sum_ref[head, at] = sum_ref[head, at] * keep + add
            max_ref[head, at] = new

    def part_in_arrival(head):
        return pltpu.make_async_remote_copy(
            src_ref=part_in_out.at[head], dst_ref=part_in.at[head],
            send_sem=pi_send.at[head], recv_sem=pi_recv.at[head],
            device_id={"ctx": base + head}, device_id_type=MESH,
        )

    def part_cross_arrival(head):
        return pltpu.make_async_remote_copy(
            src_ref=part_cross_out.at[head], dst_ref=part_cross.at[head],
            send_sem=pc_send.at[head], recv_sem=pc_recv.at[head],
            device_id={"ctx": base - GROUP + head}, device_id_type=MESH,
        )

    def part_lone_arrival(which, head):
        return pltpu.make_async_remote_copy(
            src_ref=part_lone_out, dst_ref=part_lone.at[which, head],
            send_sem=pl_send, recv_sem=pl_recv.at[which, head],
            device_id={"ctx": (1 - which) * GROUP + head}, device_id_type=MESH,
        )

    @pl.when(z > 0)
    def _():
        def body(head, carry):
            @pl.when(head != z)
            def _():
                part_in_arrival(head).wait_recv()

            merge(head, part_in[head], N_SUB)
            return carry

        lax.fori_loop(0, N_HEAD, body, 0)

    @pl.when((x == 2) & (z == 0))
    def _():
        def body(head, carry):
            for which in range(2):
                part_lone_arrival(which, head).wait_recv()
                merge(head, part_lone[which, head], 2)
            return carry

        lax.fori_loop(0, N_HEAD, body, 0)

    @pl.when(is_odd)
    def _():
        def body(head, carry):
            part_cross_arrival(head).wait_recv()
            merge(head, part_cross[head], N_SUB)
            return carry

        lax.fori_loop(0, N_HEAD, body, 0)

    for side in range(2):
        for place, step in enumerate((2, 1, 3, 0)):
            owner = lax.rem(y + step, 4) * 2 + (1 - core if side == 0 else core)
            rows = pl.ds(pl.multiple_of(owner * ROWS, ROWS), ROWS)
            for head in range(N_HEAD):
                att_ref[side, place * ROWS : (place + 1) * ROWS, head * HEAD : (head + 1) * HEAD] = (
                    acc_ref[head, rows] / sum_ref[head, rows]
                ).astype(BF16)
    weight_load.wait()

    def sided(t):
        sign = 1 - 2 * lax.rem(t, 2)
        onward = lax.rem(y + sign + 4, 4) * 2 + core
        back = lax.rem(y - sign + 4, 4) * 2 + core
        return onward, back

    def columns(t):
        return pl.ds(pl.multiple_of((t // 2) * COLS + lax.rem(t, 2) * (MODEL // 2), COLS), COLS)

    def remote(source, target, send_sem, recv_sem, t, other):
        return pltpu.make_async_remote_copy(
            src_ref=source.at[t], dst_ref=target.at[t], send_sem=send_sem.at[t], recv_sem=recv_sem.at[t],
            device_id={"head": other}, device_id_type=MESH,
        )

    def send_pair(t):
        return remote(pair_out, pair_in, pair_send, pair_recv, t, others[0])

    def send_far(t):
        return remote(far_out, far_in, far_send, far_recv, t, sided(t)[0])

    def send_relay(t):
        return remote(relay_out, relay_in, relay_send, relay_recv, t, sided(t)[0])

    def send_near(t):
        return remote(near_out, near_in, near_send, near_recv, t, sided(t)[1])

    def project(t, carry):
        @pl.when(t < N_COLS)
        def _():
            weights = w_ref[:, columns(t)]
            pair_out[t] = nn(att_ref[0], weights).astype(BF16)
            send_pair(t).start()
            mine_ref[t] = nn(att_ref[1], weights)

        @pl.when((t >= 1) & (t < N_COLS + 1))
        def _():
            p = t - 1
            send_pair(p).wait_recv()
            both = mine_ref[p] + pair_in[p].astype(F32)
            up = lax.rem(p, 2) == 0
            one, two = both[ROWS : 2 * ROWS], both[2 * ROWS : 3 * ROWS]
            far_out[p] = both[0:ROWS].astype(BF16)
            send_far(p).start()
            near_out[p] = jnp.where(up, two, one).astype(BF16)
            send_near(p).start()
            mine_ref[p, 0:ROWS] = jnp.where(up, one, two)
            mine_ref[p, 3 * ROWS :] = both[3 * ROWS :]

        @pl.when(t >= 3)
        def _():
            p = t - 3
            send_far(p).wait_recv()
            relay_out[p] = (mine_ref[p, 0:ROWS] + far_in[p].astype(F32)).astype(BF16)
            send_relay(p).start()

        return carry

    lax.fori_loop(0, N_COLS + 3, project, 0)

    def finish(t, carry):
        send_near(t).wait_recv()
        send_relay(t).wait_recv()
        total = mine_ref[t, 3 * ROWS :] + near_in[t].astype(F32) + relay_in[t].astype(F32)
        out_ref[:, columns(t)] = total.astype(BF16)
        send_pair(t).wait_send()
        send_far(t).wait_send()
        send_near(t).wait_send()
        send_relay(t).wait_send()
        return carry

    lax.fori_loop(0, N_COLS, finish, 0)

    for slot in range(GROUP):
        @pl.when(slot != z)
        def _():
            send_packet(slot, z).wait_send()
            send_keys(slot, z).wait_send()
            send_values(slot, z).wait_send()

        @pl.when(is_odd)
        def _():
            send_forward(slot).wait_send()

        @pl.when(jnp.logical_not(is_odd))
        def _():
            send_part_cross(slot).wait_send()

        if slot > 0:
            @pl.when(slot != z)
            def _():
                send_part_in(slot).wait_send()

    @pl.when((x == 1) | (x == 2))
    def _():
        send_lone().wait_send()

    @pl.when(x < 2)
    def _():
        send_part_lone(0).wait_send()


def layer(queries, keys, values, vectors, logits, docs, out_weight):
    part = lambda *shape: pltpu.VMEM(shape, BF16)
    wide = lambda *shape: pltpu.VMEM(shape, F32)
    dma = lambda *shape: pltpu.SemaphoreType.DMA(shape)
    return pl.pallas_call(
        layer_kernel,
        out_shape=jax.ShapeDtypeStruct((ROWS, MODEL), BF16),
        in_specs=[pl.BlockSpec(memory_space=pl.ANY)] * 4
        + [pl.BlockSpec(memory_space=pltpu.VMEM)] * 2
        + [pl.BlockSpec(memory_space=pl.ANY)],
        out_specs=pl.BlockSpec(memory_space=pltpu.VMEM),
        scratch_shapes=[
            *[part(N_HEAD, BLOCK, HEAD)] * 4, part(BLOCK, MODEL),
            part(7, SUB, SUB), wide(N_HEAD, BLOCK), part(N_HEAD, PACKET, HEAD), part(GROUP, PACKET, HEAD),
            part(N_HEAD, BLOCK, HEAD), part(GROUP, BLOCK, HEAD), part(GROUP, BLOCK, HEAD), wide(N_HEAD, 10, SUB, SUB),
            part(6, BLOCK, HEAD), part(GROUP, PART, HEAD), part(GROUP, PART, HEAD), part(TILE, HEAD), part(TILE, HEAD),
            part(GROUP, PART, HEAD), part(GROUP, PART, HEAD), part(PART_HALF, HEAD), part(N_HEAD, PART, HEAD),
            part(N_HEAD, PART, HEAD), part(2, N_HEAD, PART_HALF, HEAD), wide(2, 2, SUB),
            wide(N_HEAD, BLOCK, HEAD), wide(N_HEAD, BLOCK, HEAD), wide(N_HEAD, BLOCK, HEAD),
            part(2, TILE, BLOCK), wide(N_COLS, TILE, COLS), part(N_COLS, TILE, COLS), part(N_COLS, TILE, COLS),
            *[part(N_COLS, ROWS, COLS)] * 6,
            dma(4, N_HEAD), pltpu.SemaphoreType.DMA,
            dma(3), *[dma(GROUP)] * 6, dma(GROUP), dma(GROUP),
            pltpu.SemaphoreType.DMA, pltpu.SemaphoreType.DMA,
            dma(GROUP), dma(GROUP), dma(GROUP), dma(GROUP), pltpu.SemaphoreType.DMA, dma(2, GROUP),
            *[dma(N_COLS)] * 8,
        ],
        compiler_params=pltpu.CompilerParams(
            collective_id=0, has_side_effects=True, vmem_limit_bytes=60 * 1024 * 1024
        ),
    )(queries, keys, values, vectors, logits, docs, out_weight)


def on_device(queries, keys, values, vectors, logits, docs, out_weight):
    return layer(queries, keys, values, vectors, logits.T, docs.reshape(N_SUB, SUB), out_weight)


def solution(mesh):
    return jax.shard_map(
        on_device,
        mesh=mesh,
        in_specs=(
            P("ctx", "head"),
            P("ctx", "head"),
            P("ctx", "head"),
            P("ctx", "head"),
            P("ctx", "head"),
            P("ctx"),
            P("head", None),
        ),
        out_specs=P(("ctx", "head"), None),
        check_vma=False,
    )
```

```python
import math

import jax
import jax.numpy as jnp
from jax import lax
from jax.experimental import pallas as pl
from jax.experimental.pallas import tpu as pltpu
from jax.sharding import PartitionSpec as P

MESH = pl.DeviceIdType.MESH
F32 = jnp.float32
BF16 = jnp.bfloat16

HEAD = 128
BLOCK = 512
SUB = 128
N_SUB = 4
N_HEAD = 4
GROUP = 4
TILE = 256
COLS = 1024
N_COLS = 8
ROWS = 32
OWNERS = 8
MODEL = 4096
NEG = -1e30
TRIANGLE = (0, 1, 3, 6)
UNIT = math.log2(math.e) / math.sqrt(HEAD)

TOGETHER = 2
PAIRED = 2
AT_Q, AT_T, AT_D = 0, 512, 640
PACKET = 656
FORWARD = 16 + BLOCK
PART = TILE + 16


def nn(a, b):
    return lax.dot_general(a, b, (((1,), (0,)), ((), ())), preferred_element_type=F32)


def nt(a, b):
    return lax.dot_general(a, b, (((1,), (1,)), ((), ())), preferred_element_type=F32)


def halves(a):
    high = a.astype(BF16)
    return high, (a - high.astype(F32)).astype(BF16)


def rows_to_column(row, eye):
    return jnp.sum(jnp.where(eye, row, 0.0), axis=1, keepdims=True)


def column_to_rows(column, eye):
    return jnp.sum(jnp.where(eye, column, 0.0), axis=0, keepdims=True)


def pieces(rows):
    high = rows.astype(BF16).astype(F32)
    rest = rows - high
    middle = rest.astype(BF16).astype(F32)
    low = rest - middle
    pad = jnp.zeros((16 - 3 * rows.shape[0], rows.shape[1]), F32)
    return jnp.concatenate([high, middle, low, pad], axis=0).astype(BF16)


def unpieced(tail, count):
    tail = tail.astype(F32)
    return tail[:count] + tail[count : 2 * count] + tail[2 * count : 3 * count]


def identity_masks():
    row = lax.broadcasted_iota(jnp.int32, (SUB, SUB), 0)
    col = lax.broadcasted_iota(jnp.int32, (SUB, SUB), 1)
    return row, col


def layer_kernel(
    q_hbm, k_hbm, v_hbm, u_hbm, logit_ref, doc_ref, w_hbm, out_ref,
    q_ref, k_ref, v_ref, u_ref, w_ref, level_ref, beta_ref, packet_out, packet_in, keys_out, keys_in, values_in, score_ref,
    z_ref, y_ref, step_ref, near_ref, far_ref, pair_ref, turned_ref, early_ref, end_ref, forward_ref, cross_in, lone_in, lone_out,
    part_in_out, part_cross_out, part_lone_out, part_in, part_cross, part_lone,
    acc_ref, max_ref, sum_ref,
    att_ref, mine_ref, pair_out, pair_in, far_out, far_in, relay_out, relay_in, near_out, near_in,
    load_sem, w_sem, own_sem, pk_send, pk_recv, ks_send, ks_recv, vs_send, vs_recv, xf_send, xf_recv, lone_send, lone_recv,
    pi_send, pi_recv, pc_send, pc_recv, pl_send, pl_recv,
    pair_send, pair_recv, far_send, far_recv, relay_send, relay_recv, near_send, near_recv,
):
    me = lax.axis_index("ctx")
    n_ctx = lax.axis_size("ctx")
    x = me // GROUP
    z = lax.rem(me, GROUP)
    base = x * GROUP

    here = lax.axis_index("head")
    y = here // 2
    core = lax.rem(here, 2)

    barrier = pltpu.get_barrier_semaphore()
    others = [y * 2 + 1 - core] + [lax.rem(y + step, 4) * 2 + core for step in (1, 3)]
    for other in others:
        pl.semaphore_signal(barrier, inc=1, device_id={"head": other}, device_id_type=MESH)

    def greet(step, carry):
        pl.semaphore_signal(barrier, inc=1, device_id={"ctx": lax.rem(me + step, n_ctx)}, device_id_type=MESH)
        return carry

    lax.fori_loop(1, n_ctx, greet, 0)

    def load(index, head):
        source = (q_hbm, k_hbm, v_hbm, u_hbm)[index]
        target = (q_ref, k_ref, v_ref, u_ref)[index]
        lanes = pl.ds(pl.multiple_of(head * HEAD, HEAD), HEAD)
        return pltpu.make_async_copy(source.at[:, lanes], target.at[head], load_sem.at[index, head])

    def start_loads(turn, carry):
        for index in range(4):
            load(index, lax.rem(z + 1 + turn, N_HEAD)).start()
        return carry

    lax.fori_loop(0, N_HEAD, start_loads, 0)
    weight_load = pltpu.make_async_copy(w_hbm, w_ref, w_sem)
    weight_load.start()

    row, col = identity_masks()
    for level in range(7):
        hit = ((row >> level) + 1 == (col >> level)) & (((row >> level) & 1) == 0)
        level_ref[level] = jnp.where(hit, 1.0, 0.0).astype(BF16)
    beta_ref[...] = 2.0 * jax.nn.sigmoid(logit_ref[...])

    def to_group(source, target, send_sem, recv_sem, head, slot):
        return pltpu.make_async_remote_copy(
            src_ref=source.at[head], dst_ref=target.at[slot],
            send_sem=send_sem.at[head], recv_sem=recv_sem.at[slot],
            device_id={"ctx": base + head}, device_id_type=MESH,
        )

    def send_packet(head, slot):
        return to_group(packet_out, packet_in, pk_send, pk_recv, head, slot)

    def send_keys(head, slot):
        return to_group(keys_out, keys_in, ks_send, ks_recv, head, slot)

    def send_values(head, slot):
        return to_group(v_ref, values_in, vs_send, vs_recv, head, slot)

    def wait_value_load(turn, carry):
        load(2, lax.rem(z + 1 + turn, N_HEAD)).wait()
        return carry

    lax.fori_loop(0, N_HEAD, wait_value_load, 0)
    own_values = pltpu.make_async_copy(v_ref.at[z], values_in.at[z], own_sem.at[0])
    own_values.start()
    pl.semaphore_wait(barrier, n_ctx - 1 + len(others))

    def start_values(turn, carry):
        send_values(lax.rem(z + 1 + turn, N_HEAD), z).start()
        return carry

    lax.fori_loop(0, N_HEAD - 1, start_values, 0)

    def as_b(value):
        return value.astype(BF16)

    def beside(*parts):
        return jnp.concatenate(parts, axis=1)

    def below(*parts):
        return jnp.concatenate(parts, axis=0)

    def product(left, right):
        left_high, left_low = halves(left)
        right_high, right_low = halves(right)
        return nn(beside(left_high, left_low, left_high), below(right_high, right_high, right_low))

    subs = range(N_SUB * TOGETHER)
    starts = range(0, N_SUB * TOGETHER, N_SUB)
    sub_rows = [slice(a * SUB, (a + 1) * SUB) for a in range(N_SUB)]

    def heads_of(turn):
        return [lax.rem(z + 1 + turn * TOGETHER + i, N_HEAD) for i in range(TOGETHER)]

    def store_tiles(target, head, first, value):
        for i in range(value.shape[0] // (2 * ROWS)):
            for tile in range(2):
                to = tile * TILE + (first + i) * ROWS
                target[head, to : to + ROWS] = value[(2 * i + tile) * ROWS : (2 * i + tile + 1) * ROWS]

    def query_step(turn, carry):
        heads = heads_of(turn)
        row, col = identity_masks()
        eye = row == col
        upper = col > row
        causal = col <= row
        one = jnp.where(eye, 1.0, 0.0)
        for head in heads:
            for index in (0, 1, 3):
                load(index, head).wait()
        each = [(head, rows) for head in heads for rows in sub_rows]
        betas = [beta_ref[pl.ds(head, 1), :] for head in heads]
        beta = [row[:, rows] for row in betas for rows in sub_rows]
        q = [q_ref[head, rows] for head, rows in each]
        u = [u_ref[head, rows] for head, rows in each]
        tau_row, lt, lt_low, dots = [], [], [], []
        for a in subs:
            wide = u[a].astype(F32)
            tau = rows_to_column(beta[a], eye) / (jnp.sum(wide * wide, axis=1, keepdims=True) + 1e-6)
            tau_row.append(column_to_rows(tau, eye))
            grams = nt(below(u[a], q[a]), u[a])
            dots.append(jnp.where(causal, grams[SUB:], 0.0) * tau_row[a])
            high, low = halves(jnp.where(upper, grams[:SUB] * tau, 0.0))
            lt.append(high)
            lt_low.append(low)
        inverse = []
        for a in subs:
            inverse.append((one - (lt[a] * level_ref[0]).astype(F32)).astype(BF16))
        for level in range(1, 7):
            first = [nn(inverse[a], lt[a] * level_ref[level]).astype(BF16) for a in subs]
            inverse = [
                (inverse[a].astype(F32) - nn(first[a], inverse[a])).astype(BF16) for a in subs
            ]
        residual = []
        for a in subs:
            both = nn(below(lt[a], lt_low[a]), inverse[a])
            residual.append((one - inverse[a].astype(F32) - (both[:SUB] + both[SUB:])).astype(BF16))
        solved = [inverse[a].astype(F32) + nn(inverse[a], residual[a]) for a in subs]
        trans, turned, z_full = [], [], []
        for a in subs:
            high, low = halves(solved[a] * tau_row[a])
            z_full.append(nn(beside(high, low), below(u[a], u[a])))
        for a in subs:
            head, rows = each[a]
            high, low = halves(z_full[a])
            across = u[a].astype(F32).T.astype(BF16)
            trans.append(one - nn(beside(across, across), below(high, low)))
            z_ref[head, rows] = high
        for a in subs:
            head, rows = each[a]
            a_high, a_low = halves(dots[a])
            s_high, s_low = halves(solved[a])
            y = nt(beside(a_high, a_low, a_high), beside(s_high, s_high, s_low)).astype(BF16)
            y_ref[head, rows] = y
            turned.append(as_b((q[a].astype(F32) - nn(y, u[a])) * UNIT))
        for a in subs:
            head, rows = each[a]
            step_ref[head, rows] = as_b(trans[a])
            near_ref[head, rows] = turned[a]
        pair = {}
        for c in starts:
            for a in (c, c + 2):
                turned[a + 1] = as_b(nt(turned[a + 1], as_b(trans[a])))
                pair[a] = product(trans[a], trans[a + 1])
        docs = doc_ref[...].astype(F32)
        docs_tail = as_b(below(docs, jnp.zeros((16 - N_SUB, SUB), F32)))
        for head, c in zip(heads, starts):
            late = below(turned[c + 2], turned[c + 3])
            far_ref[head] = late
            store_tiles(packet_out, head, 0, below(turned[c], turned[c + 1]))
            store_tiles(packet_out, head, OWNERS // 2, as_b(nt(late, as_b(pair[c]))))
            packet_out[head, AT_T : AT_T + 128] = as_b(product(pair[c], pair[c + 2]))
            packet_out[head, AT_D : AT_D + 16] = docs_tail
            pair_ref[head] = as_b(pair[c + 2])

            @pl.when(head != z)
            def _():
                send_packet(head, z).start()

        return carry

    def key_step(turn, carry):
        heads = heads_of(turn)
        row, col = identity_masks()
        upper = col > row
        lower = col < row
        each = [(head, rows) for head in heads for rows in sub_rows]
        q = [q_ref[head, rows] for head, rows in each]
        k = [k_ref[head, rows] for head, rows in each]
        u = [u_ref[head, rows] for head, rows in each]
        keys = []
        for a in subs:
            head, rows = each[a]
            skew_t = jnp.where(upper, nt(k[a], u[a]), 0.0).astype(BF16)
            keys.append(as_b(k[a].astype(F32) - nn(skew_t, z_ref[head, rows])))
        for a in subs:
            head, rows = each[a]
            grams = nt(below(u[a], q[a]), k[a])
            skew = jnp.where(lower, grams[:SUB], 0.0).astype(BF16)
            at = a % N_SUB
            score_ref[head, TRIANGLE[at] + at] = (grams[SUB:] - nn(y_ref[head, rows], skew)) * UNIT
        for head, c in zip(heads, starts):
            for a in (0, 2):
                score_ref[head, TRIANGLE[a + 1] + a] = nt(near_ref[head, sub_rows[a + 1]], keys[c + a])
                keys[c + a] = as_b(nn(keys[c + a], step_ref[head, sub_rows[a + 1]]))
        for head, c in zip(heads, starts):
            early = below(keys[c], keys[c + 1])
            far = nt(far_ref[head], early)
            keys_out[head, 0:256] = as_b(nn(early, pair_ref[head]))
            keys_out[head, 256:512] = below(keys[c + 2], keys[c + 3])
            for a in (2, 3):
                for b in (0, 1):
                    score_ref[head, TRIANGLE[a] + b] = far[(a - 2) * SUB : (a - 1) * SUB, b * SUB : (b + 1) * SUB]

            @pl.when(head != z)
            def _():
                send_keys(head, z).start()

        return carry

    lax.fori_loop(0, N_HEAD // TOGETHER, query_step, 0)
    lax.fori_loop(0, N_HEAD // TOGETHER, key_step, 0)

    own_packet = pltpu.make_async_copy(packet_out.at[z], packet_in.at[z], own_sem.at[1])
    own_packet.start()
    own_keys = pltpu.make_async_copy(keys_out.at[z], keys_in.at[z], own_sem.at[2])
    own_keys.start()

    def own_attention(head, carry):
        row, col = identity_masks()
        eye = row == col
        causal = col <= row
        docs = doc_ref[...].astype(F32)
        for a in range(N_SUB):
            mine = rows_to_column(docs[a : a + 1], eye)
            scores = []
            for b in range(a + 1):
                allowed = mine == docs[b : b + 1]
                if b == a:
                    allowed = allowed & causal
                scores.append(jnp.where(allowed, score_ref[head, TRIANGLE[a] + b], NEG))
            top = scores[0]
            for score in scores[1:]:
                top = jnp.maximum(top, score)
            top = jnp.max(top, axis=1, keepdims=True)
            weights = [jnp.exp2(score - top) for score in scores]
            total = weights[0]
            for weight in weights[1:]:
                total = total + weight
            total = jnp.sum(total, axis=1, keepdims=True)
            joined = jnp.concatenate([as_b(weight) for weight in weights], axis=1)
            store_tiles(acc_ref, head, 2 * a, nn(joined, v_ref[head, 0 : (a + 1) * SUB]))
            store_tiles(max_ref, head, 2 * a, jnp.broadcast_to(top, (SUB, HEAD)))
            store_tiles(sum_ref, head, 2 * a, jnp.broadcast_to(total, (SUB, HEAD)))
        return carry

    own_packet.wait()
    for slot in range(GROUP):
        @pl.when(slot != z)
        def _():
            send_packet(slot, slot).wait_recv()

    def transition(slot):
        return packet_in[slot, AT_T : AT_T + 128]

    def send_forward(slot, tile):
        rows = pl.ds(0, 16 + TILE) if tile == 0 else pl.ds(16 + TILE, TILE)
        return pltpu.make_async_remote_copy(
            src_ref=forward_ref.at[slot, rows], dst_ref=cross_in.at[slot, rows],
            send_sem=xf_send.at[tile, slot], recv_sem=xf_recv.at[tile, slot],
            device_id={"ctx": lax.rem(me + n_ctx - GROUP, n_ctx)}, device_id_type=MESH,
        )

    def send_lone():
        return pltpu.make_async_remote_copy(
            src_ref=lone_out, dst_ref=lone_in,
            send_sem=lone_send, recv_sem=lone_recv,
            device_id={"ctx": lax.rem(me + n_ctx - GROUP, n_ctx)}, device_id_type=MESH,
        )

    @pl.when(x == 2)
    def _():
        lone_out[...] = below(packet_in[0, 0:SUB], packet_in[0, TILE : TILE + SUB])
        send_lone().start()

    is_odd = lax.rem(x, 2) == 1
    trans = [transition(slot) for slot in range(GROUP)]
    pair_low = as_b(nn(trans[0], trans[1]))
    pair_high = as_b(nn(trans[2], trans[3]))
    turned_last = as_b(nt(packet_in[3, 0:BLOCK], trans[2]))
    turned_ref[...] = turned_last
    for slot in range(GROUP):
        forward_ref[slot, 0:16] = packet_in[slot, AT_D : AT_D + 16]
    forward_ref[0, 16:] = packet_in[0, 0:BLOCK]
    forward_ref[1, 16:] = as_b(nt(packet_in[1, 0:BLOCK], trans[0]))
    forward_ref[2, 16:] = as_b(nt(packet_in[2, 0:BLOCK], pair_low))
    forward_ref[3, 16:] = as_b(nt(turned_last, pair_low))

    @pl.when(is_odd)
    def _():
        for slot in range(GROUP):
            send_forward(slot, 0).start()

    lax.fori_loop(0, N_HEAD, own_attention, 0)

    @pl.when(x == 1)
    def _():
        send_lone().wait_recv()
        lone_out[...] = as_b(nt(lone_in[...], as_b(nn(pair_low, pair_high))))
        send_lone().start()

    @pl.when(is_odd)
    def _():
        for slot in range(GROUP):
            send_forward(slot, 1).start()

    row, col = identity_masks()
    eye = row == col

    own_values.wait()
    own_keys.wait()
    for slot in range(GROUP):
        @pl.when(slot != z)
        def _():
            send_values(slot, slot).wait_recv()
            send_keys(slot, slot).wait_recv()

    early_ref[0:BLOCK] = as_b(nn(keys_in[0], trans[1]))
    early_ref[BLOCK:] = keys_in[1]
    end_ref[0 : 2 * BLOCK] = as_b(nn(early_ref[...], pair_high))
    end_ref[2 * BLOCK : 3 * BLOCK] = as_b(nn(keys_in[2], trans[3]))
    end_ref[3 * BLOCK :] = keys_in[3]

    def key_documents(first, last):
        rows = []
        for slot in range(first, last):
            docs = packet_in[slot, AT_D : AT_D + 16].astype(F32)
            rows += [docs[a : a + 1] for a in range(N_SUB)]
        return rows

    def attend(pieces_of_keys, query_docs):
        scores = []
        for value, keys, first, last in pieces_of_keys:
            raw = nt(value, keys)
            for a, docs in enumerate(key_documents(first, last)):
                scores.append(jnp.where(query_docs == docs, raw[:, a * SUB : (a + 1) * SUB], NEG))
        top = scores[0]
        for score in scores[1:]:
            top = jnp.maximum(top, score)
        top = jnp.max(top, axis=1, keepdims=True)
        weights = [jnp.exp2(score - top) for score in scores]
        total = weights[0]
        for weight in weights[1:]:
            total = total + weight
        total = jnp.sum(total, axis=1, keepdims=True)
        mixed = None
        at = 0
        for _, _, first, last in pieces_of_keys:
            count = (last - first) * N_SUB
            joined = jnp.concatenate([as_b(weight) for weight in weights[at : at + count]], axis=1)
            at += count
            values = jnp.concatenate([values_in[slot] for slot in range(first, last)], axis=0)
            term = nn(joined, values)
            mixed = term if mixed is None else mixed + term
        return as_b(mixed / total), top + jnp.log2(total)

    def query_documents(docs, tile):
        columns = [rows_to_column(docs[a : a + 1], eye) for a in range(N_SUB)]
        return jnp.concatenate(
            [
                columns[owner // 2][(2 * (owner % 2) + tile) * ROWS : (2 * (owner % 2) + tile + 1) * ROWS]
                for owner in range(OWNERS)
            ],
            axis=0,
        )

    def log_rows(log_sum):
        return jnp.concatenate(
            [column_to_rows(log_sum[a * SUB : (a + 1) * SUB], eye) for a in range(2)], axis=0
        )

    def send_part_in(slot):
        return pltpu.make_async_remote_copy(
            src_ref=part_in_out.at[slot], dst_ref=part_in.at[z],
            send_sem=pi_send.at[slot], recv_sem=pi_recv.at[z],
            device_id={"ctx": base + slot}, device_id_type=MESH,
        )

    def send_part_lone(which):
        return pltpu.make_async_remote_copy(
            src_ref=part_lone_out, dst_ref=part_lone.at[which, z],
            send_sem=pl_send, recv_sem=pl_recv.at[which, z],
            device_id={"ctx": 2 * GROUP}, device_id_type=MESH,
        )

    def lone_rows():
        mixed, log_sum = attend([(lone_in[...], end_ref[...], 0, GROUP)], jnp.zeros((TILE, 1), F32))
        part_lone_out[0:TILE] = mixed
        part_lone_out[TILE:] = pieces(log_rows(log_sum))
        send_part_lone(1 - x).start()

    @pl.when(x == 1)
    def _():
        lone_rows()

    def send_part_in(slot, tile):
        return pltpu.make_async_remote_copy(
            src_ref=part_in_out.at[tile, slot], dst_ref=part_in.at[tile, z],
            send_sem=pi_send.at[tile, slot], recv_sem=pi_recv.at[tile, z],
            device_id={"ctx": base + slot}, device_id_type=MESH,
        )

    for tile in range(2):
        at = slice(tile * TILE, (tile + 1) * TILE)
        work = {
            1: [(packet_in[1, at], keys_in[0], 0, 1)],
            2: [(packet_in[2, at], early_ref[...], 0, 2)],
            3: [(packet_in[3, at], keys_in[2], 2, 3), (turned_ref[at], early_ref[...], 0, 2)],
        }
        for slot, parts in work.items():
            docs = packet_in[slot, AT_D : AT_D + 16].astype(F32)
            mixed, log_sum = attend(parts, query_documents(docs, tile))
            part_in_out[tile, slot, 0:TILE] = mixed
            part_in_out[tile, slot, TILE:] = pieces(log_rows(log_sum))
        for slot in work:
            @pl.when(slot != z)
            def _():
                send_part_in(slot, tile).start()

            @pl.when(slot == z)
            def _():
                part_in[tile, z] = part_in_out[tile, slot]

    def send_part_cross(slot, tile):
        return pltpu.make_async_remote_copy(
            src_ref=part_cross_out.at[tile, slot], dst_ref=part_cross.at[tile, z],
            send_sem=pc_send.at[tile, slot], recv_sem=pc_recv.at[tile, z],
            device_id={"ctx": lax.rem(base + GROUP + slot, n_ctx)}, device_id_type=MESH,
        )

    def cross(step, tile):
        slots = [step * PAIRED + i for i in range(PAIRED)]
        for slot in slots:
            send_forward(slot, tile).wait_recv()
        for slot in slots:
            docs = cross_in[slot, 0:16].astype(F32)
            value = cross_in[slot, 16 + tile * TILE : 16 + (tile + 1) * TILE]
            mixed, log_sum = attend([(value, end_ref[...], 0, GROUP)], query_documents(docs, tile))
            part_cross_out[tile, slot, 0:TILE] = mixed
            part_cross_out[tile, slot, TILE:] = pieces(log_rows(log_sum))
        for slot in slots:
            send_part_cross(slot, tile).start()

    @pl.when(x == 0)
    def _():
        send_lone().wait_recv()
        lone_rows()

    @pl.when(jnp.logical_not(is_odd))
    def _():
        for tile in range(2):
            def body(step, carry):
                cross(step, tile)
                return carry

            lax.fori_loop(0, GROUP // PAIRED, body, 0)


    def merge(head, at, values, log_row):
        log_sum = rows_to_column(log_row, eye)
        old = max_ref[head, at]
        new = jnp.maximum(old, log_sum)
        keep = jnp.exp2(old - new)
        add = jnp.exp2(log_sum - new)
        acc_ref[head, at] = acc_ref[head, at] * keep + values.astype(F32) * add
        sum_ref[head, at] = sum_ref[head, at] * keep + add
        max_ref[head, at] = new

    def merge_tile(head, tile, part):
        logs = unpieced(part[TILE:], 2)
        for i in range(2):
            at = slice(tile * TILE + i * SUB, tile * TILE + (i + 1) * SUB)
            merge(head, at, part[i * SUB : (i + 1) * SUB], logs[i : i + 1])

    def part_arrival(source, target, send_sem, recv_sem, tile, head, device):
        return pltpu.make_async_remote_copy(
            src_ref=source.at[tile, head], dst_ref=target.at[tile, head],
            send_sem=send_sem.at[tile, head], recv_sem=recv_sem.at[tile, head],
            device_id={"ctx": device}, device_id_type=MESH,
        )

    def part_lone_arrival(which, head):
        return pltpu.make_async_remote_copy(
            src_ref=part_lone_out, dst_ref=part_lone.at[which, head],
            send_sem=pl_send, recv_sem=pl_recv.at[which, head],
            device_id={"ctx": (1 - which) * GROUP + head}, device_id_type=MESH,
        )

    def gather(tile):
        @pl.when(z > 0)
        def _():
            def body(head, carry):
                @pl.when(head != z)
                def _():
                    part_arrival(part_in_out, part_in, pi_send, pi_recv, tile, head, base + head).wait_recv()

                merge_tile(head, tile, part_in[tile, head])
                return carry

            lax.fori_loop(0, N_HEAD, body, 0)

        @pl.when((x == 2) & (z == 0))
        def _():
            def body(head, carry):
                for which in range(2):
                    if tile == 0:
                        part_lone_arrival(which, head).wait_recv()
                    part = part_lone[which, head]
                    logs = unpieced(part[TILE:], 2)
                    at = slice(tile * TILE, tile * TILE + SUB)
                    merge(head, at, part[tile * SUB : (tile + 1) * SUB], logs[tile : tile + 1])
                return carry

            lax.fori_loop(0, N_HEAD, body, 0)

        @pl.when(is_odd)
        def _():
            def body(head, carry):
                part_arrival(
                    part_cross_out, part_cross, pc_send, pc_recv, tile, head, base - GROUP + head
                ).wait_recv()
                merge_tile(head, tile, part_cross[tile, head])
                return carry

            lax.fori_loop(0, N_HEAD, body, 0)

        for side in range(2):
            for place, step in enumerate((2, 1, 3, 0)):
                owner = lax.rem(y + step, 4) * 2 + (1 - core if side == 0 else core)
                rows = pl.ds(pl.multiple_of(tile * TILE + owner * ROWS, ROWS), ROWS)
                to = side * SUB + place * ROWS
                for head in range(N_HEAD):
                    att_ref[tile, to : to + ROWS, head * HEAD : (head + 1) * HEAD] = (
                        acc_ref[head, rows] / sum_ref[head, rows]
                    ).astype(BF16)

    weight_load.wait()
    gather(0)

    def sided(t):
        sign = 1 - 2 * lax.rem(t, 2)
        onward = lax.rem(y + sign + 4, 4) * 2 + core
        back = lax.rem(y - sign + 4, 4) * 2 + core
        return onward, back

    def columns(t):
        return pl.ds(pl.multiple_of((lax.rem(t, 4) // 2) * COLS + lax.rem(t, 2) * (MODEL // 2), COLS), COLS)

    def remote(source, target, send_sem, recv_sem, t, other):
        return pltpu.make_async_remote_copy(
            src_ref=source.at[t], dst_ref=target.at[t], send_sem=send_sem.at[t], recv_sem=recv_sem.at[t],
            device_id={"head": other}, device_id_type=MESH,
        )

    def send_pair(t):
        return remote(pair_out, pair_in, pair_send, pair_recv, t, others[0])

    def send_far(t):
        return remote(far_out, far_in, far_send, far_recv, t, sided(t)[0])

    def send_relay(t):
        return remote(relay_out, relay_in, relay_send, relay_recv, t, sided(t)[0])

    def send_near(t):
        return remote(near_out, near_in, near_send, near_recv, t, sided(t)[1])

    def project(t, carry):
        @pl.when((t >= 1) & (t < N_COLS + 1))
        def _():
            p = t - 1
            send_pair(p).wait_recv()
            both = mine_ref[p] + pair_in[p].astype(F32)
            up = lax.rem(p, 2) == 0
            one, two = both[ROWS : 2 * ROWS], both[2 * ROWS : 3 * ROWS]
            far_out[p] = both[0:ROWS].astype(BF16)
            send_far(p).start()
            near_out[p] = jnp.where(up, two, one).astype(BF16)
            send_near(p).start()
            mine_ref[p, 0:ROWS] = jnp.where(up, one, two)
            mine_ref[p, 3 * ROWS :] = both[3 * ROWS :]

        @pl.when(t == N_COLS // 2)
        def _():
            gather(1)

        @pl.when(t >= 3)
        def _():
            p = t - 3
            send_far(p).wait_recv()
            relay_out[p] = (mine_ref[p, 0:ROWS] + far_in[p].astype(F32)).astype(BF16)
            send_relay(p).start()

        @pl.when(t < N_COLS)
        def _():
            product = nn(att_ref[t // (N_COLS // 2)], w_ref[:, columns(t)])
            pair_out[t] = product[:SUB].astype(BF16)
            send_pair(t).start()
            mine_ref[t] = product[SUB:]

        return carry

    lax.fori_loop(0, N_COLS + 3, project, 0)

    def finish(t, carry):
        send_near(t).wait_recv()
        send_relay(t).wait_recv()
        total = mine_ref[t, 3 * ROWS :] + near_in[t].astype(F32) + relay_in[t].astype(F32)
        rows = pl.ds(pl.multiple_of((t // (N_COLS // 2)) * ROWS, ROWS), ROWS)
        out_ref[rows, columns(t)] = total.astype(BF16)
        send_pair(t).wait_send()
        send_far(t).wait_send()
        send_near(t).wait_send()
        send_relay(t).wait_send()
        return carry

    lax.fori_loop(0, N_COLS, finish, 0)

    for slot in range(GROUP):
        @pl.when(slot != z)
        def _():
            send_packet(slot, z).wait_send()
            send_keys(slot, z).wait_send()
            send_values(slot, z).wait_send()

        for tile in range(2):
            @pl.when(is_odd)
            def _():
                send_forward(slot, tile).wait_send()

            @pl.when(jnp.logical_not(is_odd))
            def _():
                send_part_cross(slot, tile).wait_send()

            if slot > 0:
                @pl.when(slot != z)
                def _():
                    send_part_in(slot, tile).wait_send()

    @pl.when((x == 1) | (x == 2))
    def _():
        send_lone().wait_send()

    @pl.when(x < 2)
    def _():
        send_part_lone(0).wait_send()


def layer(queries, keys, values, vectors, logits, docs, out_weight):
    part = lambda *shape: pltpu.VMEM(shape, BF16)
    wide = lambda *shape: pltpu.VMEM(shape, F32)
    dma = lambda *shape: pltpu.SemaphoreType.DMA(shape)
    return pl.pallas_call(
        layer_kernel,
        out_shape=jax.ShapeDtypeStruct((2 * ROWS, MODEL), BF16),
        in_specs=[pl.BlockSpec(memory_space=pl.ANY)] * 4
        + [pl.BlockSpec(memory_space=pltpu.VMEM)] * 2
        + [pl.BlockSpec(memory_space=pl.ANY)],
        out_specs=pl.BlockSpec(memory_space=pltpu.VMEM),
        scratch_shapes=[
            *[part(N_HEAD, BLOCK, HEAD)] * 4, part(BLOCK, MODEL),
            part(7, SUB, SUB), wide(N_HEAD, BLOCK), part(N_HEAD, PACKET, HEAD), part(GROUP, PACKET, HEAD),
            part(N_HEAD, BLOCK, HEAD), part(GROUP, BLOCK, HEAD), part(GROUP, BLOCK, HEAD), wide(N_HEAD, 10, SUB, SUB),
            *[part(N_HEAD, BLOCK, HEAD)] * 4, part(N_HEAD, TILE, HEAD), part(N_HEAD, SUB, HEAD),
            part(BLOCK, HEAD), part(2 * BLOCK, HEAD), part(4 * BLOCK, HEAD), part(GROUP, FORWARD, HEAD), part(GROUP, FORWARD, HEAD), part(TILE, HEAD), part(TILE, HEAD),
            part(2, GROUP, PART, HEAD), part(2, GROUP, PART, HEAD), part(PART, HEAD), part(2, N_HEAD, PART, HEAD),
            part(2, N_HEAD, PART, HEAD), part(2, N_HEAD, PART, HEAD),
            wide(N_HEAD, BLOCK, HEAD), wide(N_HEAD, BLOCK, HEAD), wide(N_HEAD, BLOCK, HEAD),
            part(2, TILE, BLOCK), wide(N_COLS, SUB, COLS), part(N_COLS, SUB, COLS), part(N_COLS, SUB, COLS),
            *[part(N_COLS, ROWS, COLS)] * 6,
            dma(4, N_HEAD), pltpu.SemaphoreType.DMA,
            dma(3), *[dma(GROUP)] * 6, dma(2, GROUP), dma(2, GROUP),
            pltpu.SemaphoreType.DMA, pltpu.SemaphoreType.DMA,
            *[dma(2, GROUP)] * 4, pltpu.SemaphoreType.DMA, dma(2, GROUP),
            *[dma(N_COLS)] * 8,
        ],
        compiler_params=pltpu.CompilerParams(
            collective_id=0, has_side_effects=True, vmem_limit_bytes=60 * 1024 * 1024
        ),
    )(queries, keys, values, vectors, logits, docs, out_weight)


def on_device(queries, keys, values, vectors, logits, docs, out_weight):
    return layer(queries, keys, values, vectors, logits.T, docs.reshape(N_SUB, SUB), out_weight)


def solution(mesh):
    return jax.shard_map(
        on_device,
        mesh=mesh,
        in_specs=(
            P("ctx", "head"),
            P("ctx", "head"),
            P("ctx", "head"),
            P("ctx", "head"),
            P("ctx", "head"),
            P("ctx"),
            P("head", None),
        ),
        out_specs=P(("ctx", "head"), None),
        check_vma=False,
    )
```

```python
import math

import jax
import jax.numpy as jnp
from jax import lax
from jax.experimental import pallas as pl
from jax.experimental.pallas import tpu as pltpu
from jax.sharding import PartitionSpec as P

MESH = pl.DeviceIdType.MESH
F32 = jnp.float32
BF16 = jnp.bfloat16

HEAD = 128
BLOCK = 512
SUB = 128
N_SUB = 4
N_HEAD = 4
GROUP = 4
TILE = 256
COLS = 1024
N_COLS = 8
ROWS = 32
OWNERS = 8
MODEL = 4096
NEG = -1e30
TRIANGLE = (0, 1, 3, 6)
UNIT = math.log2(math.e) / math.sqrt(HEAD)

TOGETHER = 2
PAIRED = 2
AT_Q, AT_T, AT_D = 0, 512, 640
PACKET = 656
FORWARD = 16 + BLOCK
PART = TILE + 16


def nn(a, b):
    return lax.dot_general(a, b, (((1,), (0,)), ((), ())), preferred_element_type=F32)


def nt(a, b):
    return lax.dot_general(a, b, (((1,), (1,)), ((), ())), preferred_element_type=F32)


def halves(a):
    high = a.astype(BF16)
    return high, (a - high.astype(F32)).astype(BF16)


def rows_to_column(row, eye):
    return jnp.sum(jnp.where(eye, row, 0.0), axis=1, keepdims=True)


def column_to_rows(column, eye):
    return jnp.sum(jnp.where(eye, column, 0.0), axis=0, keepdims=True)


def pieces(rows):
    high = rows.astype(BF16).astype(F32)
    rest = rows - high
    middle = rest.astype(BF16).astype(F32)
    low = rest - middle
    pad = jnp.zeros((16 - 3 * rows.shape[0], rows.shape[1]), F32)
    return jnp.concatenate([high, middle, low, pad], axis=0).astype(BF16)


def unpieced(tail, count):
    tail = tail.astype(F32)
    return tail[:count] + tail[count : 2 * count] + tail[2 * count : 3 * count]


def identity_masks():
    row = lax.broadcasted_iota(jnp.int32, (SUB, SUB), 0)
    col = lax.broadcasted_iota(jnp.int32, (SUB, SUB), 1)
    return row, col


def layer_kernel(
    q_hbm, k_hbm, v_hbm, u_hbm, logit_ref, doc_ref, w_hbm, out_ref,
    q_ref, k_ref, v_ref, u_ref, w_ref, level_ref, beta_ref, packet_out, packet_in, keys_out, keys_in, values_in, score_ref,
    z_ref, y_ref, step_ref, near_ref, far_ref, pair_ref, turned_ref, early_ref, end_ref, forward_ref, cross_in, lone_in, lone_out,
    part_in_out, part_cross_out, part_lone_out, part_in, part_cross, part_lone,
    acc_ref, max_ref, sum_ref,
    att_ref, mine_ref, pair_out, pair_in, far_out, far_in, relay_out, relay_in, near_out, near_in,
    load_sem, w_sem, own_sem, pk_send, pk_recv, ks_send, ks_recv, vs_send, vs_recv, xf_send, xf_recv, lone_send, lone_recv,
    pi_send, pi_recv, pc_send, pc_recv, pl_send, pl_recv,
    pair_send, pair_recv, far_send, far_recv, relay_send, relay_recv, near_send, near_recv,
):
    me = lax.axis_index("ctx")
    n_ctx = lax.axis_size("ctx")
    x = me // GROUP
    z = lax.rem(me, GROUP)
    base = x * GROUP

    here = lax.axis_index("head")
    y = here // 2
    core = lax.rem(here, 2)

    barrier = pltpu.get_barrier_semaphore()
    others = [y * 2 + 1 - core] + [lax.rem(y + step, 4) * 2 + core for step in (1, 3)]
    for other in others:
        pl.semaphore_signal(barrier, inc=1, device_id={"head": other}, device_id_type=MESH)

    def greet(step, carry):
        pl.semaphore_signal(barrier, inc=1, device_id={"ctx": lax.rem(me + step, n_ctx)}, device_id_type=MESH)
        return carry

    lax.fori_loop(1, n_ctx, greet, 0)

    def load(index, head):
        source = (q_hbm, k_hbm, v_hbm, u_hbm)[index]
        target = (q_ref, k_ref, v_ref, u_ref)[index]
        lanes = pl.ds(pl.multiple_of(head * HEAD, HEAD), HEAD)
        return pltpu.make_async_copy(source.at[:, lanes], target.at[head], load_sem.at[index, head])

    def start_loads(turn, carry):
        for index in range(4):
            load(index, lax.rem(z + 1 + turn, N_HEAD)).start()
        return carry

    lax.fori_loop(0, N_HEAD, start_loads, 0)
    weight_load = pltpu.make_async_copy(w_hbm, w_ref, w_sem)
    weight_load.start()

    row, col = identity_masks()
    for level in range(7):
        hit = ((row >> level) + 1 == (col >> level)) & (((row >> level) & 1) == 0)
        level_ref[level] = jnp.where(hit, 1.0, 0.0).astype(BF16)
    beta_ref[...] = 2.0 * jax.nn.sigmoid(logit_ref[...])

    def to_group(source, target, send_sem, recv_sem, head, slot):
        return pltpu.make_async_remote_copy(
            src_ref=source.at[head], dst_ref=target.at[slot],
            send_sem=send_sem.at[head], recv_sem=recv_sem.at[slot],
            device_id={"ctx": base + head}, device_id_type=MESH,
        )

    def send_packet(head, slot):
        return to_group(packet_out, packet_in, pk_send, pk_recv, head, slot)

    def send_keys(head, slot):
        return to_group(keys_out, keys_in, ks_send, ks_recv, head, slot)

    def send_values(head, slot):
        return to_group(v_ref, values_in, vs_send, vs_recv, head, slot)

    def wait_value_load(turn, carry):
        load(2, lax.rem(z + 1 + turn, N_HEAD)).wait()
        return carry

    lax.fori_loop(0, N_HEAD, wait_value_load, 0)
    own_values = pltpu.make_async_copy(v_ref.at[z], values_in.at[z], own_sem.at[0])
    own_values.start()
    pl.semaphore_wait(barrier, n_ctx - 1 + len(others))

    def start_values(turn, carry):
        send_values(lax.rem(z + 1 + turn, N_HEAD), z).start()
        return carry

    lax.fori_loop(0, N_HEAD - 1, start_values, 0)

    def as_b(value):
        return value.astype(BF16)

    def beside(*parts):
        return jnp.concatenate(parts, axis=1)

    def below(*parts):
        return jnp.concatenate(parts, axis=0)

    def product(left, right):
        left_high, left_low = halves(left)
        right_high, right_low = halves(right)
        return nn(beside(left_high, left_low, left_high), below(right_high, right_high, right_low))

    subs = range(N_SUB * TOGETHER)
    starts = range(0, N_SUB * TOGETHER, N_SUB)
    sub_rows = [slice(a * SUB, (a + 1) * SUB) for a in range(N_SUB)]

    def heads_of(turn):
        return [lax.rem(z + 1 + turn * TOGETHER + i, N_HEAD) for i in range(TOGETHER)]

    def store_tiles(target, head, first, value):
        for i in range(value.shape[0] // (2 * ROWS)):
            for tile in range(2):
                to = tile * TILE + (first + i) * ROWS
                target[head, to : to + ROWS] = value[(2 * i + tile) * ROWS : (2 * i + tile + 1) * ROWS]

    def query_step(turn, carry):
        heads = heads_of(turn)
        row, col = identity_masks()
        eye = row == col
        upper = col > row
        causal = col <= row
        one = jnp.where(eye, 1.0, 0.0)
        for head in heads:
            for index in (0, 1, 3):
                load(index, head).wait()
        each = [(head, rows) for head in heads for rows in sub_rows]
        betas = [beta_ref[pl.ds(head, 1), :] for head in heads]
        beta = [row[:, rows] for row in betas for rows in sub_rows]
        q = [q_ref[head, rows] for head, rows in each]
        u = [u_ref[head, rows] for head, rows in each]
        tau_row, lt, lt_low, dots = [], [], [], []
        for a in subs:
            wide = u[a].astype(F32)
            tau = rows_to_column(beta[a], eye) / (jnp.sum(wide * wide, axis=1, keepdims=True) + 1e-6)
            tau_row.append(column_to_rows(tau, eye))
            grams = nt(below(u[a], q[a]), u[a])
            dots.append(jnp.where(causal, grams[SUB:], 0.0) * tau_row[a])
            high, low = halves(jnp.where(upper, grams[:SUB] * tau, 0.0))
            lt.append(high)
            lt_low.append(low)
        inverse = []
        for a in subs:
            inverse.append((one - (lt[a] * level_ref[0]).astype(F32)).astype(BF16))
        for level in range(1, 7):
            first = [nn(inverse[a], lt[a] * level_ref[level]).astype(BF16) for a in subs]
            inverse = [
                (inverse[a].astype(F32) - nn(first[a], inverse[a])).astype(BF16) for a in subs
            ]
        residual = []
        for a in subs:
            both = nn(below(lt[a], lt_low[a]), inverse[a])
            residual.append((one - inverse[a].astype(F32) - (both[:SUB] + both[SUB:])).astype(BF16))
        solved = [inverse[a].astype(F32) + nn(inverse[a], residual[a]) for a in subs]
        trans, turned, z_full = [], [], []
        for a in subs:
            high, low = halves(solved[a] * tau_row[a])
            z_full.append(nn(beside(high, low), below(u[a], u[a])))
        for a in subs:
            head, rows = each[a]
            high, low = halves(z_full[a])
            across = u[a].astype(F32).T.astype(BF16)
            trans.append(one - nn(beside(across, across), below(high, low)))
            z_ref[head, rows] = high
        for a in subs:
            head, rows = each[a]
            a_high, a_low = halves(dots[a])
            s_high, s_low = halves(solved[a])
            y = nt(beside(a_high, a_low, a_high), beside(s_high, s_high, s_low)).astype(BF16)
            y_ref[head, rows] = y
            turned.append(as_b((q[a].astype(F32) - nn(y, u[a])) * UNIT))
        for a in subs:
            head, rows = each[a]
            step_ref[head, rows] = as_b(trans[a])
            near_ref[head, rows] = turned[a]
        pair = {}
        for c in starts:
            for a in (c, c + 2):
                turned[a + 1] = as_b(nt(turned[a + 1], as_b(trans[a])))
                pair[a] = product(trans[a], trans[a + 1])
        docs = doc_ref[...].astype(F32)
        docs_tail = as_b(below(docs, jnp.zeros((16 - N_SUB, SUB), F32)))
        for head, c in zip(heads, starts):
            late = below(turned[c + 2], turned[c + 3])
            far_ref[head] = late
            store_tiles(packet_out, head, 0, below(turned[c], turned[c + 1]))
            store_tiles(packet_out, head, OWNERS // 2, as_b(nt(late, as_b(pair[c]))))
            packet_out[head, AT_T : AT_T + 128] = as_b(product(pair[c], pair[c + 2]))
            packet_out[head, AT_D : AT_D + 16] = docs_tail
            pair_ref[head] = as_b(pair[c + 2])

            @pl.when(head != z)
            def _():
                send_packet(head, z).start()

        return carry

    def key_step(turn, carry):
        heads = heads_of(turn)
        row, col = identity_masks()
        upper = col > row
        lower = col < row
        each = [(head, rows) for head in heads for rows in sub_rows]
        q = [q_ref[head, rows] for head, rows in each]
        k = [k_ref[head, rows] for head, rows in each]
        u = [u_ref[head, rows] for head, rows in each]
        keys = []
        for a in subs:
            head, rows = each[a]
            skew_t = jnp.where(upper, nt(k[a], u[a]), 0.0).astype(BF16)
            keys.append(as_b(k[a].astype(F32) - nn(skew_t, z_ref[head, rows])))
        for a in subs:
            head, rows = each[a]
            grams = nt(below(u[a], q[a]), k[a])
            skew = jnp.where(lower, grams[:SUB], 0.0).astype(BF16)
            at = a % N_SUB
            score_ref[head, TRIANGLE[at] + at] = (grams[SUB:] - nn(y_ref[head, rows], skew)) * UNIT
        for head, c in zip(heads, starts):
            for a in (0, 2):
                score_ref[head, TRIANGLE[a + 1] + a] = nt(near_ref[head, sub_rows[a + 1]], keys[c + a])
                keys[c + a] = as_b(nn(keys[c + a], step_ref[head, sub_rows[a + 1]]))
        for head, c in zip(heads, starts):
            early = below(keys[c], keys[c + 1])
            far = nt(far_ref[head], early)
            keys_out[head, 0:256] = as_b(nn(early, pair_ref[head]))
            keys_out[head, 256:512] = below(keys[c + 2], keys[c + 3])
            for a in (2, 3):
                for b in (0, 1):
                    score_ref[head, TRIANGLE[a] + b] = far[(a - 2) * SUB : (a - 1) * SUB, b * SUB : (b + 1) * SUB]

            @pl.when(head != z)
            def _():
                send_keys(head, z).start()

        return carry

    lax.fori_loop(0, N_HEAD // TOGETHER, query_step, 0)
    lax.fori_loop(0, N_HEAD // TOGETHER, key_step, 0)

    own_packet = pltpu.make_async_copy(packet_out.at[z], packet_in.at[z], own_sem.at[1])
    own_packet.start()
    own_keys = pltpu.make_async_copy(keys_out.at[z], keys_in.at[z], own_sem.at[2])
    own_keys.start()

    def own_attention(head, carry):
        row, col = identity_masks()
        eye = row == col
        causal = col <= row
        docs = doc_ref[...].astype(F32)
        for a in range(N_SUB):
            mine = rows_to_column(docs[a : a + 1], eye)
            scores = []
            for b in range(a + 1):
                allowed = mine == docs[b : b + 1]
                if b == a:
                    allowed = allowed & causal
                scores.append(jnp.where(allowed, score_ref[head, TRIANGLE[a] + b], NEG))
            top = scores[0]
            for score in scores[1:]:
                top = jnp.maximum(top, score)
            top = jnp.max(top, axis=1, keepdims=True)
            weights = [jnp.exp2(score - top) for score in scores]
            total = weights[0]
            for weight in weights[1:]:
                total = total + weight
            total = jnp.sum(total, axis=1, keepdims=True)
            joined = jnp.concatenate([as_b(weight) for weight in weights], axis=1)
            store_tiles(acc_ref, head, 2 * a, nn(joined, v_ref[head, 0 : (a + 1) * SUB]))
            store_tiles(max_ref, head, 2 * a, jnp.broadcast_to(top, (SUB, HEAD)))
            store_tiles(sum_ref, head, 2 * a, jnp.broadcast_to(total, (SUB, HEAD)))
        return carry

    own_packet.wait()
    for slot in range(GROUP):
        @pl.when(slot != z)
        def _():
            send_packet(slot, slot).wait_recv()

    def transition(slot):
        return packet_in[slot, AT_T : AT_T + 128]

    def send_forward(slot, tile):
        rows = pl.ds(0, 16 + TILE) if tile == 0 else pl.ds(16 + TILE, TILE)
        return pltpu.make_async_remote_copy(
            src_ref=forward_ref.at[slot, rows], dst_ref=cross_in.at[slot, rows],
            send_sem=xf_send.at[tile, slot], recv_sem=xf_recv.at[tile, slot],
            device_id={"ctx": lax.rem(me + n_ctx - GROUP, n_ctx)}, device_id_type=MESH,
        )

    def send_lone():
        return pltpu.make_async_remote_copy(
            src_ref=lone_out, dst_ref=lone_in,
            send_sem=lone_send, recv_sem=lone_recv,
            device_id={"ctx": lax.rem(me + n_ctx - GROUP, n_ctx)}, device_id_type=MESH,
        )

    @pl.when(x == 2)
    def _():
        lone_out[...] = below(packet_in[0, 0:SUB], packet_in[0, TILE : TILE + SUB])
        send_lone().start()

    is_odd = lax.rem(x, 2) == 1
    trans = [transition(slot) for slot in range(GROUP)]
    pair_low = as_b(nn(trans[0], trans[1]))
    pair_high = as_b(nn(trans[2], trans[3]))
    turned_last = as_b(nt(packet_in[3, 0:BLOCK], trans[2]))
    turned_ref[...] = turned_last
    for slot in range(GROUP):
        forward_ref[slot, 0:16] = packet_in[slot, AT_D : AT_D + 16]
    forward_ref[0, 16:] = packet_in[0, 0:BLOCK]
    forward_ref[1, 16:] = as_b(nt(packet_in[1, 0:BLOCK], trans[0]))
    forward_ref[2, 16:] = as_b(nt(packet_in[2, 0:BLOCK], pair_low))
    forward_ref[3, 16:] = as_b(nt(turned_last, pair_low))

    @pl.when(is_odd)
    def _():
        for slot in range(GROUP):
            send_forward(slot, 0).start()

    lax.fori_loop(0, N_HEAD, own_attention, 0)

    @pl.when(x == 1)
    def _():
        send_lone().wait_recv()
        lone_out[...] = as_b(nt(lone_in[...], as_b(nn(pair_low, pair_high))))
        send_lone().start()

    @pl.when(is_odd)
    def _():
        for slot in range(GROUP):
            send_forward(slot, 1).start()

    row, col = identity_masks()
    eye = row == col

    own_values.wait()
    own_keys.wait()
    for slot in range(GROUP):
        @pl.when(slot != z)
        def _():
            send_values(slot, slot).wait_recv()
            send_keys(slot, slot).wait_recv()

    early_ref[0:BLOCK] = as_b(nn(keys_in[0], trans[1]))
    early_ref[BLOCK:] = keys_in[1]
    end_ref[0 : 2 * BLOCK] = as_b(nn(early_ref[...], pair_high))
    end_ref[2 * BLOCK : 3 * BLOCK] = as_b(nn(keys_in[2], trans[3]))
    end_ref[3 * BLOCK :] = keys_in[3]

    def key_documents(first, last):
        rows = []
        for slot in range(first, last):
            docs = packet_in[slot, AT_D : AT_D + 16].astype(F32)
            rows += [docs[a : a + 1] for a in range(N_SUB)]
        return rows

    def attend(pieces_of_keys, query_docs):
        scores = []
        for value, keys, first, last in pieces_of_keys:
            raw = nt(value, keys)
            for a, docs in enumerate(key_documents(first, last)):
                scores.append(jnp.where(query_docs == docs, raw[:, a * SUB : (a + 1) * SUB], NEG))
        top = scores[0]
        for score in scores[1:]:
            top = jnp.maximum(top, score)
        top = jnp.max(top, axis=1, keepdims=True)
        weights = [jnp.exp2(score - top) for score in scores]
        total = weights[0]
        for weight in weights[1:]:
            total = total + weight
        total = jnp.sum(total, axis=1, keepdims=True)
        mixed = None
        at = 0
        for _, _, first, last in pieces_of_keys:
            count = (last - first) * N_SUB
            joined = jnp.concatenate([as_b(weight) for weight in weights[at : at + count]], axis=1)
            at += count
            values = jnp.concatenate([values_in[slot] for slot in range(first, last)], axis=0)
            term = nn(joined, values)
            mixed = term if mixed is None else mixed + term
        return as_b(mixed / total), top + jnp.log2(total)

    def query_documents(docs, tile):
        columns = [rows_to_column(docs[a : a + 1], eye) for a in range(N_SUB)]
        return jnp.concatenate(
            [
                columns[owner // 2][(2 * (owner % 2) + tile) * ROWS : (2 * (owner % 2) + tile + 1) * ROWS]
                for owner in range(OWNERS)
            ],
            axis=0,
        )

    def log_rows(log_sum):
        return jnp.concatenate(
            [column_to_rows(log_sum[a * SUB : (a + 1) * SUB], eye) for a in range(2)], axis=0
        )

    def send_part_in(slot):
        return pltpu.make_async_remote_copy(
            src_ref=part_in_out.at[slot], dst_ref=part_in.at[z],
            send_sem=pi_send.at[slot], recv_sem=pi_recv.at[z],
            device_id={"ctx": base + slot}, device_id_type=MESH,
        )

    def send_part_lone(which):
        return pltpu.make_async_remote_copy(
            src_ref=part_lone_out, dst_ref=part_lone.at[which, z],
            send_sem=pl_send, recv_sem=pl_recv.at[which, z],
            device_id={"ctx": 2 * GROUP}, device_id_type=MESH,
        )

    def lone_rows():
        mixed, log_sum = attend([(lone_in[...], end_ref[...], 0, GROUP)], jnp.zeros((TILE, 1), F32))
        part_lone_out[0:TILE] = mixed
        part_lone_out[TILE:] = pieces(log_rows(log_sum))
        send_part_lone(1 - x).start()

    @pl.when(x == 1)
    def _():
        lone_rows()

    def send_part_in(slot, tile):
        return pltpu.make_async_remote_copy(
            src_ref=part_in_out.at[tile, slot], dst_ref=part_in.at[tile, z],
            send_sem=pi_send.at[tile, slot], recv_sem=pi_recv.at[tile, z],
            device_id={"ctx": base + slot}, device_id_type=MESH,
        )

    def pairs_within(tile):
        at = slice(tile * TILE, (tile + 1) * TILE)
        work = {
            1: [(packet_in[1, at], keys_in[0], 0, 1)],
            2: [(packet_in[2, at], early_ref[...], 0, 2)],
            3: [(packet_in[3, at], keys_in[2], 2, 3), (turned_ref[at], early_ref[...], 0, 2)],
        }
        for slot, parts in work.items():
            docs = packet_in[slot, AT_D : AT_D + 16].astype(F32)
            mixed, log_sum = attend(parts, query_documents(docs, tile))
            part_in_out[tile, slot, 0:TILE] = mixed
            part_in_out[tile, slot, TILE:] = pieces(log_rows(log_sum))
        for slot in work:
            @pl.when(slot != z)
            def _():
                send_part_in(slot, tile).start()

            @pl.when(slot == z)
            def _():
                part_in[tile, z] = part_in_out[tile, slot]

    def send_part_cross(slot, tile):
        return pltpu.make_async_remote_copy(
            src_ref=part_cross_out.at[tile, slot], dst_ref=part_cross.at[tile, z],
            send_sem=pc_send.at[tile, slot], recv_sem=pc_recv.at[tile, z],
            device_id={"ctx": lax.rem(base + GROUP + slot, n_ctx)}, device_id_type=MESH,
        )

    def cross(step, tile):
        slots = [step * PAIRED + i for i in range(PAIRED)]
        for slot in slots:
            send_forward(slot, tile).wait_recv()
        for slot in slots:
            docs = cross_in[slot, 0:16].astype(F32)
            value = cross_in[slot, 16 + tile * TILE : 16 + (tile + 1) * TILE]
            mixed, log_sum = attend([(value, end_ref[...], 0, GROUP)], query_documents(docs, tile))
            part_cross_out[tile, slot, 0:TILE] = mixed
            part_cross_out[tile, slot, TILE:] = pieces(log_rows(log_sum))
        for slot in slots:
            send_part_cross(slot, tile).start()

    def cross_tile(tile):
        @pl.when(jnp.logical_not(is_odd))
        def _():
            def body(step, carry):
                cross(step, tile)
                return carry

            lax.fori_loop(0, GROUP // PAIRED, body, 0)

    pairs_within(0)
    cross_tile(0)

    @pl.when(x == 0)
    def _():
        send_lone().wait_recv()
        lone_rows()

    pairs_within(1)
    cross_tile(1)


    def merge(head, at, values, log_row):
        log_sum = rows_to_column(log_row, eye)
        old = max_ref[head, at]
        new = jnp.maximum(old, log_sum)
        keep = jnp.exp2(old - new)
        add = jnp.exp2(log_sum - new)
        acc_ref[head, at] = acc_ref[head, at] * keep + values.astype(F32) * add
        sum_ref[head, at] = sum_ref[head, at] * keep + add
        max_ref[head, at] = new

    def merge_tile(head, tile, part):
        logs = unpieced(part[TILE:], 2)
        for i in range(2):
            at = slice(tile * TILE + i * SUB, tile * TILE + (i + 1) * SUB)
            merge(head, at, part[i * SUB : (i + 1) * SUB], logs[i : i + 1])

    def part_arrival(source, target, send_sem, recv_sem, tile, head, device):
        return pltpu.make_async_remote_copy(
            src_ref=source.at[tile, head], dst_ref=target.at[tile, head],
            send_sem=send_sem.at[tile, head], recv_sem=recv_sem.at[tile, head],
            device_id={"ctx": device}, device_id_type=MESH,
        )

    def part_lone_arrival(which, head):
        return pltpu.make_async_remote_copy(
            src_ref=part_lone_out, dst_ref=part_lone.at[which, head],
            send_sem=pl_send, recv_sem=pl_recv.at[which, head],
            device_id={"ctx": (1 - which) * GROUP + head}, device_id_type=MESH,
        )

    def gather(tile):
        @pl.when(z > 0)
        def _():
            def body(head, carry):
                @pl.when(head != z)
                def _():
                    part_arrival(part_in_out, part_in, pi_send, pi_recv, tile, head, base + head).wait_recv()

                merge_tile(head, tile, part_in[tile, head])
                return carry

            lax.fori_loop(0, N_HEAD, body, 0)

        @pl.when((x == 2) & (z == 0))
        def _():
            def body(head, carry):
                for which in range(2):
                    if tile == 0:
                        part_lone_arrival(which, head).wait_recv()
                    part = part_lone[which, head]
                    logs = unpieced(part[TILE:], 2)
                    at = slice(tile * TILE, tile * TILE + SUB)
                    merge(head, at, part[tile * SUB : (tile + 1) * SUB], logs[tile : tile + 1])
                return carry

            lax.fori_loop(0, N_HEAD, body, 0)

        @pl.when(is_odd)
        def _():
            def body(head, carry):
                part_arrival(
                    part_cross_out, part_cross, pc_send, pc_recv, tile, head, base - GROUP + head
                ).wait_recv()
                merge_tile(head, tile, part_cross[tile, head])
                return carry

            lax.fori_loop(0, N_HEAD, body, 0)

        for side in range(2):
            for place, step in enumerate((2, 1, 3, 0)):
                owner = lax.rem(y + step, 4) * 2 + (1 - core if side == 0 else core)
                rows = pl.ds(pl.multiple_of(tile * TILE + owner * ROWS, ROWS), ROWS)
                to = side * SUB + place * ROWS
                for head in range(N_HEAD):
                    att_ref[tile, to : to + ROWS, head * HEAD : (head + 1) * HEAD] = (
                        acc_ref[head, rows] / sum_ref[head, rows]
                    ).astype(BF16)

    weight_load.wait()
    gather(0)

    def sided(t):
        sign = 1 - 2 * lax.rem(t, 2)
        onward = lax.rem(y + sign + 4, 4) * 2 + core
        back = lax.rem(y - sign + 4, 4) * 2 + core
        return onward, back

    def columns(t):
        return pl.ds(pl.multiple_of((lax.rem(t, 4) // 2) * COLS + lax.rem(t, 2) * (MODEL // 2), COLS), COLS)

    def remote(source, target, send_sem, recv_sem, t, other):
        return pltpu.make_async_remote_copy(
            src_ref=source.at[t], dst_ref=target.at[t], send_sem=send_sem.at[t], recv_sem=recv_sem.at[t],
            device_id={"head": other}, device_id_type=MESH,
        )

    def send_pair(t):
        return remote(pair_out, pair_in, pair_send, pair_recv, t, others[0])

    def send_far(t):
        return remote(far_out, far_in, far_send, far_recv, t, sided(t)[0])

    def send_relay(t):
        return remote(relay_out, relay_in, relay_send, relay_recv, t, sided(t)[0])

    def send_near(t):
        return remote(near_out, near_in, near_send, near_recv, t, sided(t)[1])

    half = N_COLS // 2

    def stage(t, late, work):
        p = t - late

        @pl.when((p >= 0) & (p < N_COLS))
        def _():
            work(p)

    def pair_up(p):
        send_pair(p).wait_recv()
        both = mine_ref[p] + pair_in[p].astype(F32)
        up = lax.rem(p, 2) == 0
        one, two = both[ROWS : 2 * ROWS], both[2 * ROWS : 3 * ROWS]
        far_out[p] = both[0:ROWS].astype(BF16)
        send_far(p).start()
        near_out[p] = jnp.where(up, two, one).astype(BF16)
        send_near(p).start()
        mine_ref[p, 0:ROWS] = jnp.where(up, one, two)
        mine_ref[p, 3 * ROWS :] = both[3 * ROWS :]

    def relay(p):
        send_far(p).wait_recv()
        relay_out[p] = (mine_ref[p, 0:ROWS] + far_in[p].astype(F32)).astype(BF16)
        send_relay(p).start()

    def multiply(p):
        product = nn(att_ref[p // half], w_ref[:, columns(p)])
        pair_out[p] = product[:SUB].astype(BF16)
        send_pair(p).start()
        mine_ref[p] = product[SUB:]

    def project(t, carry):
        stage(t, 2, pair_up)
        stage(t, 5, relay)

        @pl.when(t == half)
        def _():
            gather(1)

        stage(t, 0, multiply)
        return carry

    lax.fori_loop(0, N_COLS + 5, project, 0)

    def finish(t, carry):
        send_near(t).wait_recv()
        send_relay(t).wait_recv()
        total = mine_ref[t, 3 * ROWS :] + near_in[t].astype(F32) + relay_in[t].astype(F32)
        rows = pl.ds(pl.multiple_of((t // (N_COLS // 2)) * ROWS, ROWS), ROWS)
        out_ref[rows, columns(t)] = total.astype(BF16)
        send_pair(t).wait_send()
        send_far(t).wait_send()
        send_near(t).wait_send()
        send_relay(t).wait_send()
        return carry

    lax.fori_loop(0, N_COLS, finish, 0)

    for slot in range(GROUP):
        @pl.when(slot != z)
        def _():
            send_packet(slot, z).wait_send()
            send_keys(slot, z).wait_send()
            send_values(slot, z).wait_send()

        for tile in range(2):
            @pl.when(is_odd)
            def _():
                send_forward(slot, tile).wait_send()

            @pl.when(jnp.logical_not(is_odd))
            def _():
                send_part_cross(slot, tile).wait_send()

            if slot > 0:
                @pl.when(slot != z)
                def _():
                    send_part_in(slot, tile).wait_send()

    @pl.when((x == 1) | (x == 2))
    def _():
        send_lone().wait_send()

    @pl.when(x < 2)
    def _():
        send_part_lone(0).wait_send()


def layer(queries, keys, values, vectors, logits, docs, out_weight):
    part = lambda *shape: pltpu.VMEM(shape, BF16)
    wide = lambda *shape: pltpu.VMEM(shape, F32)
    dma = lambda *shape: pltpu.SemaphoreType.DMA(shape)
    return pl.pallas_call(
        layer_kernel,
        out_shape=jax.ShapeDtypeStruct((2 * ROWS, MODEL), BF16),
        in_specs=[pl.BlockSpec(memory_space=pl.ANY)] * 4
        + [pl.BlockSpec(memory_space=pltpu.VMEM)] * 2
        + [pl.BlockSpec(memory_space=pl.ANY)],
        out_specs=pl.BlockSpec(memory_space=pltpu.VMEM),
        scratch_shapes=[
            *[part(N_HEAD, BLOCK, HEAD)] * 4, part(BLOCK, MODEL),
            part(7, SUB, SUB), wide(N_HEAD, BLOCK), part(N_HEAD, PACKET, HEAD), part(GROUP, PACKET, HEAD),
            part(N_HEAD, BLOCK, HEAD), part(GROUP, BLOCK, HEAD), part(GROUP, BLOCK, HEAD), wide(N_HEAD, 10, SUB, SUB),
            *[part(N_HEAD, BLOCK, HEAD)] * 4, part(N_HEAD, TILE, HEAD), part(N_HEAD, SUB, HEAD),
            part(BLOCK, HEAD), part(2 * BLOCK, HEAD), part(4 * BLOCK, HEAD), part(GROUP, FORWARD, HEAD), part(GROUP, FORWARD, HEAD), part(TILE, HEAD), part(TILE, HEAD),
            part(2, GROUP, PART, HEAD), part(2, GROUP, PART, HEAD), part(PART, HEAD), part(2, N_HEAD, PART, HEAD),
            part(2, N_HEAD, PART, HEAD), part(2, N_HEAD, PART, HEAD),
            wide(N_HEAD, BLOCK, HEAD), wide(N_HEAD, BLOCK, HEAD), wide(N_HEAD, BLOCK, HEAD),
            part(2, TILE, BLOCK), wide(N_COLS, SUB, COLS), part(N_COLS, SUB, COLS), part(N_COLS, SUB, COLS),
            *[part(N_COLS, ROWS, COLS)] * 6,
            dma(4, N_HEAD), pltpu.SemaphoreType.DMA,
            dma(3), *[dma(GROUP)] * 6, dma(2, GROUP), dma(2, GROUP),
            pltpu.SemaphoreType.DMA, pltpu.SemaphoreType.DMA,
            *[dma(2, GROUP)] * 4, pltpu.SemaphoreType.DMA, dma(2, GROUP),
            *[dma(N_COLS)] * 8,
        ],
        compiler_params=pltpu.CompilerParams(
            collective_id=0, has_side_effects=True, vmem_limit_bytes=60 * 1024 * 1024
        ),
    )(queries, keys, values, vectors, logits, docs, out_weight)


def on_device(queries, keys, values, vectors, logits, docs, out_weight):
    return layer(queries, keys, values, vectors, logits.T, docs.reshape(N_SUB, SUB), out_weight)


def solution(mesh):
    return jax.shard_map(
        on_device,
        mesh=mesh,
        in_specs=(
            P("ctx", "head"),
            P("ctx", "head"),
            P("ctx", "head"),
            P("ctx", "head"),
            P("ctx", "head"),
            P("ctx"),
            P("head", None),
        ),
        out_specs=P(("ctx", "head"), None),
        check_vma=False,
    )
```
